512 devices in a mesh: blk: 32 (over z_hi, y), tensor: 16 (over x, z_lo, core).
Axes of the slice: x: 4, y: 8, z: 8 (z_hi: 4, z_lo: 2; z = z_hi * 2 + z_lo), core: 2. Of those that a mesh axis runs over, the one named last changes fastest.
Arguments:
- tokens: bfloat16 [8192, 2560], P('blk'), may hold values from -11 to 11
- doc_ids: int32 [8192], P('blk'), may hold values from 0 to 127, never falling along the last dimension, each value on 1 to 128 neighbouring positions
- qkv_weight: bfloat16 [2560, 3, 4096], P('blk', None, 'tensor'), may hold values from -0.15811388 to 0.15811388
- out_weight: bfloat16 [4096, 2560], P('tensor', 'blk'), may hold values from -0.09375 to 0.09375
- cotangent: bfloat16 [8192, 2560], P('blk'), may hold values from -0.5 to 0.5
Outputs:
- mixed: bfloat16 [8192, 2560], P('blk')
- grad_qkv: float32 [2560, 3, 4096], P('blk', None, 'tensor')
- grad_out: float32 [4096, 2560], P('tensor', 'blk')
The draws below stay inside these ranges and needn't reach their ends.
Inputs may be any that keep to these rules, and one draw needn't show every extreme that they name: `doc_ids`: never falls along the tokens; a document holds at most half of 256 tokens, and one holds exactly that many.
All inputs are finite; a program needn't handle non-finite values.
Results may differ from the reference program's by a relative error of at most 0.028.
Values may be sent and summed in bfloat16 or wider, within the bound.
A program may use at most 64 MiB of HBM per device.

```python
import math
import jax
import jax.numpy as jnp
import numpy as np
from jax import lax

D = 2560
HEADS = 32
HD = 128
TOK = 256
TOKENS = 8192
N_BLK = 32
N_TENSOR = 16


def draw_tokens(key, part):
    key = jax.random.fold_in(key, 7)
    key_entries = jax.random.fold_in(key, 0)
    values = jnp.clip(jax.random.normal(key_entries, (TOKENS, D), jnp.float32), -4.0, 4.0)
    return values.astype(jnp.bfloat16)


def draw_qkv_weight(key, part):
    key = jax.random.fold_in(key, 11)
    raw_values = jnp.clip(jax.random.normal(key, (D, 3, HEADS * HD), jnp.float32), -5.0, 5.0)
    return (raw_values / math.sqrt(D)).astype(jnp.bfloat16)


def with_spikes(values, rng, source, target, blocks, factor):
    owner, partner = [(jnp.arange(values.shape[axis_at]) // (values.shape[axis_at] // blocks)).reshape([-1 if axis == axis_at else 1 for axis in range(values.ndim)]) for axis_at in (source, target)]
    chosen = jax.random.permutation(rng, blocks)[partner]
    strong = (owner == chosen) | (owner == (partner + blocks // 2) % blocks)
    return jnp.where(strong, factor * values, values)


def levels(stream_key, dims, cuts, least, top_value):
    factor_of = 1.0
    for dim, parts in cuts:
        heights = jax.random.uniform(jax.random.fold_in(jax.random.fold_in(stream_key, 6), dim), (parts,), jnp.float32, least / len(cuts), top_value / len(cuts))
        factor_of = factor_of * jnp.repeat(jnp.exp(heights), dims[dim] // parts).reshape((-1,) + (1,) * (len(dims) - 1 - dim))
    return factor_of


def length_profile(number_of, total, bound, lean):
    weights = [(1 << 20) // math.isqrt(standing ** lean) + 1 for standing in range(2, number_of + 1)]
    rest, holding = total - bound - (number_of - 1), [1] * (number_of - 1)
    while rest > 0:
        candidates = [i for i in range(number_of - 1) if holding[i] < bound]
        pool, left = sum([weights[i] for i in candidates]), rest
        for i in candidates:
            extra = min(bound - holding[i], max(1, left * weights[i] // pool), rest)
            holding[i] = holding[i] + extra
            rest = rest - extra
    return np.array([bound] + holding)


def uneven(stream_key, amount, total, bound, skew):
    if amount == 2:
        one = jax.random.randint(stream_key, (), max(1, total - bound), min(bound, total - 1) + 1)
        return jnp.stack([one, total - one])
    lengths = jnp.asarray(length_profile(amount, total, bound, skew), jnp.int32)
    twos = (amount - 1) // 2
    giver, sink = lengths[1:1 + 2 * twos:2], lengths[2:2 + 2 * twos:2]
    room = jnp.minimum(giver - 1, bound - sink)
    shifted = jax.random.randint(jax.random.fold_in(stream_key, 1), (twos,), 0, 1 << 20) % (room + 1)
    lengths = lengths.at[1:1 + 2 * twos:2].set(giver - shifted).at[2:2 + 2 * twos:2].set(sink + shifted)
    return lengths[jax.random.permutation(jax.random.fold_in(stream_key, 2), amount)]


def normal_values(key, dims, scale, limit, shards=(), kind=jnp.bfloat16):
    drawn = scale * jax.random.normal(key, dims, jnp.float32)
    if shards:
        drawn = drawn * levels(key, dims, shards, -0.22, 0.18)
    return jnp.clip(drawn, -limit, limit).astype(kind)


def gaussian_with(rng, dims, scale, reach, pieces, heavy, held_as=jnp.bfloat16):
    result = scale * jax.random.normal(rng, dims, jnp.float32)
    if pieces:
        result = result * levels(rng, dims, pieces, -0.22, 0.18)
    return jnp.clip(with_spikes(result, jax.random.fold_in(rng, 3), *heavy), -reach, reach).astype(held_as)


def setup_inputs(seed: int = 0) -> dict:
    key_of = jax.random.split(jax.random.key(seed), 6)
    tokens = draw_tokens(jax.random.fold_in(key_of[5], 71), 0)
    doc_ids = jnp.searchsorted(jnp.cumsum(uneven(key_of[1], 4 * N_BLK, TOKENS, TOK // 2, 1)), jnp.arange(TOKENS), side="right").astype(jnp.int32)
    qkv_weight = draw_qkv_weight(jax.random.fold_in(key_of[5], 71), 0)
    out_weight = normal_values(key_of[3], (HEADS * HD, D), (HEADS * HD) ** -0.5, 0.09375, ((0, 16), (1, 32)))
    cotangent = gaussian_with(key_of[4], (TOKENS, D), 0.04, 0.5, ((0, 32),), (0, 1, 32, 2.75))
    return dict(tokens=tokens, doc_ids=doc_ids, qkv_weight=qkv_weight, out_weight=out_weight, cotangent=cotangent)


def rotate_pairs(tensor, positions):
    half_width = tensor.shape[-1] // 2
    exponent = jnp.arange(half_width, dtype=jnp.float32) * (2.0 / tensor.shape[-1])
    frequency = jnp.exp(-math.log(10000.0) * exponent)
    angles = positions[:, None] * frequency[None, :]
    cosine = jnp.cos(angles)[:, None, :]
    sine = jnp.sin(angles)[:, None, :]
    lower = tensor[..., :half_width]
    upper = tensor[..., half_width:]
    return jnp.concatenate([lower * cosine - upper * sine, upper * cosine + lower * sine], axis=-1)

def attention_weights(query_rows, key_rows, doc_ids):
    length = query_rows.shape[0]
    positions = jnp.arange(length, dtype=jnp.float32)
    query_rot = rotate_pairs(query_rows, positions)
    key_rot = rotate_pairs(key_rows, positions)
    scores = jnp.einsum('shd,thd->hst', query_rot, key_rot, precision=lax.Precision.HIGHEST)
    scores = scores / math.sqrt(query_rows.shape[-1])
    order = jnp.arange(length, dtype=jnp.int32)
    allowed = (order[None, :] <= order[:, None]) & (doc_ids[None, :] == doc_ids[:, None])
    scores = jnp.where(allowed[None], scores, -1e+30)
    highest = lax.optimization_barrier(jnp.max(scores, axis=-1, keepdims=True))
    expo_terms = jnp.exp(scores - highest)
    return expo_terms / lax.optimization_barrier(jnp.sum(expo_terms, axis=-1, keepdims=True))

def forward_context(query_rows, key_rows, value_rows, doc_ids):
    attention = attention_weights(query_rows.astype(jnp.float32), key_rows.astype(jnp.float32), doc_ids)
    attention = attention.astype(jnp.bfloat16)
    return jnp.einsum('hst,thd->shd', attention.astype(jnp.float32), value_rows.astype(jnp.float32), precision=lax.Precision.HIGHEST)

def context_exact(query_rows, key_rows, value_rows, doc_ids):
    attention = attention_weights(query_rows, key_rows, doc_ids)
    return jnp.einsum('hst,thd->shd', attention, value_rows, precision=lax.Precision.HIGHEST)

def reference(tokens, doc_ids, qkv_weight, out_weight, cotangent):
    width = HEADS * HD
    group_width = width // N_TENSOR
    qkv_flat = qkv_weight.reshape(D, 3 * width)
    out_groups = out_weight.reshape(N_TENSOR, group_width, D).astype(jnp.float32)

    def one_batch(totals, inputs):
        batch_tokens, batch_ids, batch_cot = inputs
        joined = jnp.dot(batch_tokens, qkv_flat, preferred_element_type=jnp.float32).astype(jnp.bfloat16)
        split = joined.reshape(TOK, 3, HEADS, HD)
        query_rows = split[:, 0]
        key_rows = split[:, 1]
        value_rows = split[:, 2]
        context = forward_context(query_rows, key_rows, value_rows, batch_ids).astype(jnp.bfloat16)
        context = context.reshape(TOK, width)
        grouped = context.reshape(TOK, N_TENSOR, group_width).astype(jnp.float32)
        terms = jnp.einsum('tgw,gwd->gtd', grouped, out_groups, precision=lax.Precision.HIGHEST)
        rounded = lax.optimization_barrier(terms.astype(jnp.bfloat16)).astype(jnp.float32)
        mixed = (batch_tokens.astype(jnp.float32) + lax.optimization_barrier(jnp.sum(rounded, axis=0))).astype(jnp.bfloat16)
        back_context = jnp.dot(batch_cot, out_weight.T, preferred_element_type=jnp.float32).astype(jnp.bfloat16)

        def local_context(query_in, key_in, value_in):
            return context_exact(query_in, key_in, value_in, batch_ids)
        unused, pullback = jax.vjp(local_context, query_rows.astype(jnp.float32), key_rows.astype(jnp.float32), value_rows.astype(jnp.float32))
        grads = pullback(back_context.astype(jnp.float32).reshape(TOK, HEADS, HD))
        grad_joined = jnp.stack(grads, axis=1).astype(jnp.bfloat16).reshape(TOK, 3 * width)
        grad_rows = jnp.dot(batch_tokens.T, grad_joined, preferred_element_type=jnp.float32)
        grad_cols = jnp.dot(context.T, batch_cot, preferred_element_type=jnp.float32)
        return ((totals[0] + grad_rows, totals[1] + grad_cols), mixed)
    start = (jnp.zeros((D, 3 * width), jnp.float32), jnp.zeros((width, D), jnp.float32))
    inputs = (tokens.reshape(N_BLK, TOK, D), doc_ids.reshape(N_BLK, TOK), cotangent.reshape(N_BLK, TOK, D))
    totals, mixed = lax.scan(one_batch, start, inputs)
    return (mixed.reshape(TOKENS, D), totals[0].reshape(D, 3, width), totals[1])
```

```python
import math

import jax
import jax.numpy as jnp
import numpy as np
from jax import lax
from jax.experimental import pallas as pl
from jax.experimental.pallas import tpu as pltpu
from jax.sharding import PartitionSpec as P

HD = 128
NZ, NY = 4, 8
NX, NL, NC = 4, 2, 2
F32 = jnp.float32
BF16 = jnp.bfloat16
HIGHEST = lax.Precision.HIGHEST
NT = (((1,), (1,)), ((), ()))


def dot(a, b):
    return jnp.dot(a, b, preferred_element_type=F32)


def dot_nt(a, b):
    return lax.dot_general(a, b, NT, preferred_element_type=F32)


def turned(x, cosine, sine):
    half = x.shape[1] // 2
    swapped = jnp.concatenate([x[:, half:], x[:, :half]], axis=1)
    return x * cosine + swapped * sine


def kernel(
    tokens_hbm, cot_hbm, wq_in, wo_in, doc_col, doc_row, cos_in, sin_in,
    mixed_out, gq_out, go_out,
    tok, cot, tok_t, cot_t, wq, wo, joined, ctx, back, probs, q_rot, k_rot, grad_j,
    grad_q, grad_o, sq, rq, so, ro, zsq, zrq, zso, zro,
    part, part_c, sum_c, recv_x, sum_x, recv_l, mixed,
    load_sem, ag_ss, ag_rs, agz_ss, agz_rs, rs_ss, rs_rs, rsz_ss, rsz_rs, mx_ss, mx_rs,
):
    blk = lax.axis_index("blk")
    ten = lax.axis_index("tensor")
    zh, y = blk // NY, blk % NY
    x, rest = ten // (NL * NC), ten % (NL * NC)
    lo, core = rest // NC, rest % NC
    rows = wq_in.shape[0]
    length = tok.shape[0]

    def at_z(k):
        return (((zh + k) % NZ) * NY + y, ten)

    def at_y(step):
        return (zh * NY + (y + step + NY) % NY, ten)

    def at_x(k):
        return (blk, ((x + k) % NX) * (NL * NC) + rest)

    up, down = at_y(1), at_y(-1)
    core_peer = (blk, ten + 1 - 2 * core)
    lo_peer = (blk, ten + NC - 2 * NC * lo)

    load_tok = pltpu.make_async_copy(tokens_hbm, tok, load_sem.at[0])
    load_cot = pltpu.make_async_copy(cot_hbm, cot, load_sem.at[1])
    load_tok.start()
    load_cot.start()

    barrier = pltpu.get_barrier_semaphore()
    peers = [at_z(k) for k in (1, 2, 3)] + [up, down, core_peer, lo_peer] + [at_x(k) for k in (1, 2, 3)]
    for peer in peers:
        pl.semaphore_signal(barrier, inc=1, device_id=peer, device_id_type=pl.DeviceIdType.MESH)

    def row_at(z, yy):
        return pl.ds(pl.multiple_of((z * NY + yy) * rows, 16), rows)

    mine = row_at(zh, y)
    wq[mine, :] = wq_in[...]
    wo[mine, :] = wo_in[...]
    pl.semaphore_wait(barrier, len(peers))

    def remote(src, dst, ss, rs, peer):
        return pltpu.make_async_remote_copy(
            src_ref=src, dst_ref=dst, send_sem=ss, recv_sem=rs,
            device_id=peer, device_id_type=pl.DeviceIdType.MESH,
        )

    gathered = (wq, wo)

    def ag_z(p, k):
        w = gathered[p]
        return remote(w.at[mine, :], w.at[mine, :], agz_ss.at[p, k], agz_rs.at[p, k], at_z(k))

    def ag_z_got(p, k):
        w = gathered[p]
        here = row_at((zh - k + NZ) % NZ, y)
        return remote(w.at[here, :], w.at[here, :], agz_ss.at[p, k], agz_rs.at[p, k], at_z(k))

    def ag_y(p, way, s, j, got):
        w = gathered[p]
        sign = 1 if way == 0 else -1
        off = s + 1 if got else s
        here = row_at((zh - j + NZ) % NZ, (y - sign * off + 2 * NY) % NY)
        return remote(
            w.at[here, :], w.at[here, :], ag_ss.at[p, way, s, j], ag_rs.at[p, way, s, j],
            up if way == 0 else down,
        )

    def long_js(way):
        return (0, 2) if way == 0 else (1, 3)

    def ag_first(p):
        for k in (1, 2, 3):
            ag_z(p, k).start()

        for way in (0, 1):
            ag_y(p, way, 0, 0, False).start()

        def body(j, c):
            ag_z_got(p, j).wait_recv()
            for way in (0, 1):
                ag_y(p, way, 0, j, False).start()
            return c

        lax.fori_loop(1, NZ, body, 0)

    def ag_mid(p, s):
        def body(j, c):
            for way in (0, 1):
                ag_y(p, way, s - 1, j, True).wait_recv()
                ag_y(p, way, s, j, False).start()
            return c

        lax.fori_loop(0, NZ, body, 0)

    def ag_last(p):
        for j in range(NZ):
            for way in (0, 1):
                ag_y(p, way, 2, j, True).wait_recv()
                if j in long_js(way):
                    ag_y(p, way, 3, j, False).start()

    def ag_end(p):
        for j in range(NZ):
            for way in (0, 1):
                if j in long_js(way):
                    ag_y(p, way, 3, j, True).wait_recv()

    def ag_drain(p):
        for k in (1, 2, 3):
            ag_z(p, k).wait_send()

        def body(j, c):
            for way in (0, 1):
                for s in range(3):
                    ag_y(p, way, s, j, False).wait_send()
            return c

        lax.fori_loop(0, NZ, body, 0)
        for way in (0, 1):
            for j in long_js(way):
                ag_y(p, way, 3, j, False).wait_send()

    ag_first(0)
    load_tok.wait()
    load_cot.wait()

    def flip(i, c):
        cols = pl.ds(pl.multiple_of(i * 256, 256), 256)
        tok_t[cols, :] = tok[:, cols].T
        cot_t[cols, :] = cot[:, cols].T
        return c

    ag_mid(0, 1)
    lax.fori_loop(0, tok.shape[1] // 256, flip, 0)
    ag_mid(0, 2)
    ag_last(0)
    ag_first(1)
    ag_end(0)

    cosine, sine = cos_in[...], sin_in[...]
    scale = 1.0 / math.sqrt(HD)

    def project():
        joined[...] = dot(tok[...], wq[...]).astype(BF16)

    def attend(h):
        cols = slice(h * HD, (h + 1) * HD)
        width = 2 * HD
        qr = turned(joined[:, h * HD:(h + 1) * HD].astype(F32), cosine, sine)
        kr = turned(joined[:, width + h * HD:width + (h + 1) * HD].astype(F32), cosine, sine)
        q_rot[h] = qr
        k_rot[h] = kr
        scores = lax.dot_general(qr, kr, NT, precision=HIGHEST, preferred_element_type=F32) * scale
        row = lax.broadcasted_iota(jnp.int32, (length, length), 0)
        col = lax.broadcasted_iota(jnp.int32, (length, length), 1)
        allowed = (col <= row) & (doc_row[...] == doc_col[...])
        scores = jnp.where(allowed, scores, -1e30)
        expo = jnp.exp(scores - jnp.max(scores, axis=1, keepdims=True))
        p = expo / jnp.sum(expo, axis=1, keepdims=True)
        probs[h] = p
        values = joined[:, 2 * width + h * HD:2 * width + (h + 1) * HD]
        ctx[:, cols] = dot(p.astype(BF16), values).astype(BF16)

    def retreat(h):
        width = 2 * HD
        p = probs[h]
        d_out = back[:, h * HD:(h + 1) * HD]
        values = joined[:, 2 * width + h * HD:2 * width + (h + 1) * HD]
        d_val = jnp.dot(p.T, d_out.astype(F32), precision=HIGHEST, preferred_element_type=F32)
        d_p = dot_nt(d_out, values)
        d_s = p * (d_p - jnp.sum(p * d_p, axis=1, keepdims=True)) * scale
        d_q = jnp.dot(d_s, k_rot[h], precision=HIGHEST, preferred_element_type=F32)
        d_k = jnp.dot(d_s.T, q_rot[h], precision=HIGHEST, preferred_element_type=F32)
        grad_j[:, h * HD:(h + 1) * HD] = turned(d_q, cosine, -sine).astype(BF16)
        grad_j[:, width + h * HD:width + (h + 1) * HD] = turned(d_k, cosine, -sine).astype(BF16)
        grad_j[:, 2 * width + h * HD:2 * width + (h + 1) * HD] = d_val.astype(BF16)

    project()
    ag_mid(1, 1)
    attend(0)
    ag_mid(1, 2)
    attend(1)
    ag_last(1)

    grads, sends, recvs = (grad_q, grad_o), (sq, so), (rq, ro)
    z_sends, z_recvs = (zsq, zso), (zrq, zro)

    def rs_y(p, way, d, j):
        return remote(
            sends[p].at[way, d - 1, j], recvs[p].at[way, d - 1, j],
            rs_ss.at[p, way, d - 1, j], rs_rs.at[p, way, d - 1, j],
            up if way == 0 else down,
        )

    def rs_own(p, way, d, j):
        sign = 1 if way == 0 else -1
        return grads[p][row_at((zh - j + NZ) % NZ, (y + sign * d + NY) % NY), :]

    def rs_far(p):
        for way in (0, 1):
            for j in long_js(way):
                sends[p][way, 3, j] = rs_own(p, way, 4, j).astype(BF16)
                rs_y(p, way, 4, j).start()

    def rs_three(p):
        for j in (1, 2, 3, 0):
            for way in (0, 1):
                own = rs_own(p, way, 3, j)
                if j in long_js(way):
                    rs_y(p, way, 4, j).wait_recv()
                    own = own + recvs[p][way, 3, j].astype(F32)
                sends[p][way, 2, j] = own.astype(BF16)
                rs_y(p, way, 3, j).start()

    def rs_near(p, d):
        def body(i, c):
            j = (i + 1) % NZ
            for way in (0, 1):
                rs_y(p, way, d + 1, j).wait_recv()
                own = rs_own(p, way, d, j) + recvs[p][way, d, j].astype(F32)
                sends[p][way, d - 1, j] = own.astype(BF16)
                rs_y(p, way, d, j).start()
            return c

        lax.fori_loop(0, NZ, body, 0)

    def rs_z(p, j):
        return remote(
            z_sends[p].at[j], z_recvs[p].at[j], rsz_ss.at[p, j], rsz_rs.at[p, j], at_z(NZ - j)
        )

    def rs_here(p, j):
        for way in (0, 1):
            rs_y(p, way, 1, j).wait_recv()
        own = grads[p][row_at((zh - j + NZ) % NZ, y), :]
        return own + recvs[p][0, 0, j].astype(F32) + recvs[p][1, 0, j].astype(F32)

    def rs_out(p):
        def body(j, c):
            z_sends[p][j] = rs_here(p, j).astype(BF16)
            rs_z(p, j).start()
            return c

        lax.fori_loop(1, NZ, body, 0)

    def rs_end(p, out):
        total = rs_here(p, 0)
        for j in (1, 2, 3):
            rs_z(p, j).wait_recv()
            total = total + z_recvs[p][j].astype(F32)
        out[...] = total

    def rs_drain(p):
        for j in (1, 2, 3):
            rs_z(p, j).wait_send()

        def body(j, c):
            for way in (0, 1):
                for d in (1, 2, 3):
                    rs_y(p, way, d, j).wait_send()
            return c

        lax.fori_loop(0, NZ, body, 0)
        for way in (0, 1):
            for j in long_js(way):
                rs_y(p, way, 4, j).wait_send()

    half = length // NC
    quarter = half // NX
    eighth = quarter // NL
    half_at = pl.ds(pl.multiple_of(core * half, 16), half)
    quarter_at = pl.ds(pl.multiple_of(core * half + x * quarter, 16), quarter)
    eighth_at = pl.ds(pl.multiple_of(core * half + x * quarter + lo * eighth, 16), eighth)

    def mx_core():
        away = pl.ds(pl.multiple_of((1 - core) * half, 16), half)
        return remote(part.at[away, :], part_c, mx_ss.at[0], mx_rs.at[0], core_peer)

    def mx_x(k):
        away = pl.ds(pl.multiple_of(((x + k) % NX) * quarter, 16), quarter)
        return remote(sum_c.at[away, :], recv_x.at[k - 1], mx_ss.at[k], mx_rs.at[k], at_x(k))

    def mx_lo():
        away = pl.ds(pl.multiple_of((1 - lo) * eighth, 16), eighth)
        return remote(sum_x.at[away, :], recv_l, mx_ss.at[4], mx_rs.at[4], lo_peer)

    def back_lo(got=False):
        at = eighth_at
        if got:
            at = pl.ds(pl.multiple_of(core * half + x * quarter + (1 - lo) * eighth, 16), eighth)
        return remote(mixed.at[at, :], mixed.at[at, :], mx_ss.at[5], mx_rs.at[5], lo_peer)

    def back_x(k, got=False):
        at = quarter_at
        if got:
            at = pl.ds(pl.multiple_of(core * half + ((x - k + NX) % NX) * quarter, 16), quarter)
        return remote(mixed.at[at, :], mixed.at[at, :], mx_ss.at[5 + k], mx_rs.at[5 + k], at_x(k))

    def back_core(got=False):
        at = half_at
        if got:
            at = pl.ds(pl.multiple_of((1 - core) * half, 16), half)
        return remote(mixed.at[at, :], mixed.at[at, :], mx_ss.at[9], mx_rs.at[9], core_peer)

    def stage_x():
        mx_core().wait_recv()

        def body(i, c):
            r = pl.ds(pl.multiple_of(i * 16, 16), 16)
            there = pl.ds(pl.multiple_of(core * half + i * 16, 16), 16)
            sum_c[r, :] = (part[there, :].astype(F32) + part_c[r, :].astype(F32)).astype(BF16)
            return c

        lax.fori_loop(0, half // 16, body, 0)
        for k in (1, 2, 3):
            mx_x(k).start()

    def stage_lo():
        total = sum_c[pl.ds(pl.multiple_of(x * quarter, 16), quarter), :].astype(F32)
        for k in (1, 2, 3):
            mx_x(k).wait_recv()
            total = total + recv_x[k - 1].astype(F32)
        sum_x[...] = total.astype(BF16)
        mx_lo().start()

    def stage_back():
        mx_lo().wait_recv()
        own = sum_x[pl.ds(pl.multiple_of(lo * eighth, 16), eighth), :].astype(F32)
        total = tok[eighth_at, :].astype(F32) + (own + recv_l[...].astype(F32))
        mixed[eighth_at, :] = total.astype(BF16)
        back_lo().start()

    def stage_back_x():
        back_lo(True).wait_recv()
        for k in (1, 2, 3):
            back_x(k).start()

    def stage_back_core():
        for k in (1, 2, 3):
            back_x(k, True).wait_recv()
        back_core().start()

    def widen(i, c):
        r = pl.ds(pl.multiple_of(i * 512, 512), 512)
        grad_o[r, :] = dot(cot_t[r, :], ctx[...])
        return c

    def widen_q(i, c):
        r = pl.ds(pl.multiple_of(i * 512, 512), 512)
        grad_q[r, :] = dot(tok_t[r, :], grad_j[...])
        return c

    def outward(i, c):
        r = pl.ds(pl.multiple_of(i * 512, 512), 512)
        part[:, r] = dot_nt(ctx[...], wo[r, :]).astype(BF16)
        return c

    chunks = tok.shape[1] // 512
    lax.fori_loop(0, chunks, widen, 0)
    rs_far(1)
    ag_end(1)
    lax.fori_loop(0, chunks, outward, 0)
    mx_core().start()
    rs_three(1)
    back[...] = dot(cot[...], wo[...]).astype(BF16)
    retreat(0)
    rs_near(1, 2)
    retreat(1)
    lax.fori_loop(0, chunks, widen_q, 0)
    rs_far(0)
    rs_near(1, 1)
    stage_x()
    rs_three(0)
    rs_out(1)
    stage_lo()
    rs_near(0, 2)
    stage_back()
    rs_near(0, 1)
    stage_back_x()
    rs_out(0)
    stage_back_core()
    rs_end(1, go_out)
    rs_end(0, gq_out)
    back_core(True).wait_recv()
    mixed_out[...] = mixed[...]

    for p in (0, 1):
        ag_drain(p)
        rs_drain(p)
    mx_core().wait_send()
    mx_lo().wait_send()
    back_lo().wait_send()
    back_core().wait_send()
    for k in (1, 2, 3):
        mx_x(k).wait_send()
        back_x(k).wait_send()


def local(tokens, doc_ids, qkv_weight, out_weight, cotangent):
    length, width = tokens.shape
    rows, _, feature = qkv_weight.shape
    joined_width = 3 * feature
    heads = feature // HD
    frequency = 10000.0 ** (-2.0 * np.arange(HD // 2) / HD)
    angles = np.arange(length)[:, None] * frequency[None, :]
    cosine = jnp.asarray(np.concatenate([np.cos(angles), np.cos(angles)], axis=1), F32)
    sine = jnp.asarray(np.concatenate([-np.sin(angles), np.sin(angles)], axis=1), F32)
    vmem = pl.BlockSpec(memory_space=pltpu.VMEM)
    hbm = pl.BlockSpec(memory_space=pl.ANY)
    dma = pltpu.SemaphoreType.DMA
    half = length // NC
    mixed, grad_q, grad_o = pl.pallas_call(
        kernel,
        out_shape=(
            jax.ShapeDtypeStruct((length, width), BF16),
            jax.ShapeDtypeStruct((rows, joined_width), F32),
            jax.ShapeDtypeStruct((rows, feature), F32),
        ),
        in_specs=[hbm, hbm] + [vmem] * 6,
        out_specs=(vmem, vmem, vmem),
        scratch_shapes=[
            pltpu.VMEM((length, width), BF16),
            pltpu.VMEM((length, width), BF16),
            pltpu.VMEM((width, length), BF16),
            pltpu.VMEM((width, length), BF16),
            pltpu.VMEM((width, joined_width), BF16),
            pltpu.VMEM((width, feature), BF16),
            pltpu.VMEM((length, joined_width), BF16),
            pltpu.VMEM((length, feature), BF16),
            pltpu.VMEM((length, feature), BF16),
            pltpu.VMEM((heads, length, length), F32),
            pltpu.VMEM((heads, length, HD), F32),
            pltpu.VMEM((heads, length, HD), F32),
            pltpu.VMEM((length, joined_width), BF16),
            pltpu.VMEM((width, joined_width), F32),
            pltpu.VMEM((width, feature), F32),
            pltpu.VMEM((2, 4, NZ, rows, joined_width), BF16),
            pltpu.VMEM((2, 4, NZ, rows, joined_width), BF16),
            pltpu.VMEM((2, 4, NZ, rows, feature), BF16),
            pltpu.VMEM((2, 4, NZ, rows, feature), BF16),
            pltpu.VMEM((NZ, rows, joined_width), BF16),
            pltpu.VMEM((NZ, rows, joined_width), BF16),
            pltpu.VMEM((NZ, rows, feature), BF16),
            pltpu.VMEM((NZ, rows, feature), BF16),
            pltpu.VMEM((length, width), BF16),
            pltpu.VMEM((half, width), BF16),
            pltpu.VMEM((half, width), BF16),
            pltpu.VMEM((NX - 1, half // NX, width), BF16),
            pltpu.VMEM((half // NX, width), BF16),
            pltpu.VMEM((half // NX // NL, width), BF16),
            pltpu.VMEM((length, width), BF16),
            dma((2,)),
            dma((2, 2, 4, NZ)),
            dma((2, 2, 4, NZ)),
            dma((2, NZ)),
            dma((2, NZ)),
            dma((2, 2, 4, NZ)),
            dma((2, 2, 4, NZ)),
            dma((2, NZ)),
            dma((2, NZ)),
            dma((10,)),
            dma((10,)),
        ],
        compiler_params=pltpu.CompilerParams(
            collective_id=0, has_side_effects=True, vmem_limit_bytes=56 * 1024 * 1024
        ),
        name="layer",
    )(
        tokens,
        cotangent,
        qkv_weight.reshape(rows, joined_width),
        out_weight.T,
        doc_ids.reshape(length, 1),
        doc_ids.reshape(1, length),
        cosine,
        sine,
    )
    return mixed, grad_q.reshape(rows, 3, feature), grad_o.T


def solution(mesh):
    placed = (
        P("blk", None),
        P("blk"),
        P("blk", None, "tensor"),
        P("tensor", "blk"),
        P("blk", None),
    )
    return jax.shard_map(
        local,
        mesh=mesh,
        in_specs=placed,
        out_specs=(P("blk", None), P("blk", None, "tensor"), P("tensor", "blk")),
        check_vma=False,
    )
```

```python
import math

import jax
import jax.numpy as jnp
import numpy as np
from jax import lax
from jax.experimental import pallas as pl
from jax.experimental.pallas import tpu as pltpu
from jax.sharding import PartitionSpec as P

HD = 128
NZ, NY = 4, 8
NX, NL, NC = 4, 2, 2
F32 = jnp.float32
BF16 = jnp.bfloat16
HIGHEST = lax.Precision.HIGHEST
NT = (((1,), (1,)), ((), ()))


def dot(a, b):
    return jnp.dot(a, b, preferred_element_type=F32)


def dot_nt(a, b):
    return lax.dot_general(a, b, NT, preferred_element_type=F32)


def turned(x, cosine, sine):
    half = x.shape[1] // 2
    swapped = jnp.concatenate([x[:, half:], x[:, :half]], axis=1)
    return x * cosine + swapped * sine


def kernel(
    tokens_hbm, cot_hbm, wq_in, wo_in, doc_row, cos_in, sin_in,
    mixed_out, gq_out, go_out,
    tok, cot, tok_t, cot_t, wq, wo, joined, ctx, back, probs, q_rot, k_rot, grad_j,
    grad_q, grad_o, sq, rq, so, ro, zsq, zrq, zso, zro, doc_col,
    part, part_c, sum_c, recv_x, sum_x, recv_l, mixed,
    load_sem, ag_ss, ag_rs, agz_ss, agz_rs, rs_ss, rs_rs, rsz_ss, rsz_rs,
    go_ss, go_rs, goz_ss, goz_rs, gr_ss, gr_rs, grz_ss, grz_rs, mx_ss, mx_rs,
):
    blk = lax.axis_index("blk")
    ten = lax.axis_index("tensor")
    zh, y = blk // NY, blk % NY
    x, rest = ten // (NL * NC), ten % (NL * NC)
    lo, core = rest // NC, rest % NC
    rows, third = wq_in.shape[1], wq_in.shape[2]
    length = tok.shape[0]

    def at_z(k):
        return (((zh + k) % NZ) * NY + y, ten)

    def at_y(step):
        return (zh * NY + (y + step + NY) % NY, ten)

    def at_x(k):
        return (blk, ((x + k) % NX) * (NL * NC) + rest)

    up, down = at_y(1), at_y(-1)
    core_peer = (blk, ten + 1 - 2 * core)
    lo_peer = (blk, ten + NC - 2 * NC * lo)

    load_tok = pltpu.make_async_copy(tokens_hbm, tok, load_sem.at[0])
    load_cot = pltpu.make_async_copy(cot_hbm, cot, load_sem.at[1])
    load_tok.start()
    load_cot.start()

    barrier = pltpu.get_barrier_semaphore()
    peers = [at_z(k) for k in (1, 2, 3)] + [up, down, core_peer, lo_peer] + [at_x(k) for k in (1, 2, 3)]
    for peer in peers:
        pl.semaphore_signal(barrier, inc=1, device_id=peer, device_id_type=pl.DeviceIdType.MESH)

    def row_at(z, yy):
        return pl.ds(pl.multiple_of((z * NY + yy) * rows, 16), rows)

    mine = row_at(zh, y)
    for c in range(3):
        wq[mine, c * third:(c + 1) * third] = wq_in[c]
    wo[mine, :] = wo_in[...]
    pl.semaphore_wait(barrier, len(peers))

    def remote(src, dst, ss, rs, peer):
        return pltpu.make_async_remote_copy(
            src_ref=src, dst_ref=dst, send_sem=ss, recv_sem=rs,
            device_id=peer, device_id_type=pl.DeviceIdType.MESH,
        )

    def long(way, j):
        return j % 2 == way

    def ag_z(k):
        return remote(wq.at[mine, :], wq.at[mine, :], agz_ss.at[k], agz_rs.at[k], at_z(k))

    def ag_y(way, s, j, got):
        sign = 1 if way == 0 else -1
        off = s + 1 if got else s
        here = row_at((zh - j + NZ) % NZ, (y - sign * off + 2 * NY) % NY)
        return remote(
            wq.at[here, :], wq.at[here, :], ag_ss.at[way, s, j], ag_rs.at[way, s, j],
            up if way == 0 else down,
        )

    def ag_step(j, s):
        if s == 0 and j > 0:
            here = row_at((zh - j + NZ) % NZ, y)
            remote(wq.at[here, :], wq.at[here, :], agz_ss.at[j], agz_rs.at[j], at_z(j)).wait_recv()
        for way in (0, 1):
            if s > 0:
                ag_y(way, s - 1, j, True).wait_recv()
            if s < 3 or long(way, j):
                ag_y(way, s, j, False).start()

    def ag_end():
        for j in range(NZ):
            for way in (0, 1):
                if long(way, j):
                    ag_y(way, 3, j, True).wait_recv()

    def ag_drain():
        for k in (1, 2, 3):
            ag_z(k).wait_send()
        for j in range(NZ):
            for way in (0, 1):
                for s in range(4):
                    if s < 3 or long(way, j):
                        ag_y(way, s, j, False).wait_send()

    def go_y(way, s, got):
        sign = 1 if way == 0 else -1
        off = s + 1 if got else s
        here = row_at(zh, (y - sign * off + NY) % NY)
        return remote(
            wo.at[here, :], wo.at[here, :], go_ss.at[way, s], go_rs.at[way, s],
            up if way == 0 else down,
        )

    def go_z(r, k, got=False):
        yy = (y - r + NY) % NY
        here = row_at((zh - k + NZ) % NZ if got else zh, yy)
        return remote(
            wo.at[here, :], wo.at[here, :], goz_ss.at[r, k], goz_rs.at[r, k], at_z(k)
        )

    def go_step(s):
        for way in (0, 1):
            if s > 0 and (s < 4 or way == 0):
                go_y(way, s - 1, True).wait_recv()
            if s < (4, 3)[way]:
                go_y(way, s, False).start()

    def go_spread(s):
        for r in (s,) if s in (0, 4) else (s, NY - s):
            for k in (1, 3, 2):
                go_z(r, k).start()

    def go_end():
        def body(r, c):
            for k in (1, 2, 3):
                go_z(r, k, True).wait_recv()
            return c

        lax.fori_loop(0, NY, body, 0)

    def go_drain():
        for way in (0, 1):
            for s in range((4, 3)[way]):
                go_y(way, s, False).wait_send()

        def body(r, c):
            for k in (1, 2, 3):
                go_z(r, k).wait_send()
            return c

        lax.fori_loop(0, NY, body, 0)

    ag_z(1).start()
    ag_z(3).start()
    ag_step(0, 0)
    ag_z(2).start()
    go_step(0)
    load_tok.wait()
    load_cot.wait()

    def flip(i, c):
        cols = pl.ds(pl.multiple_of(i * 256, 256), 256)
        tok_t[cols, :] = tok[:, cols].T
        cot_t[cols, :] = cot[:, cols].T
        return c

    ag_step(0, 1)
    go_step(1)
    ag_step(1, 0)
    lax.fori_loop(0, tok.shape[1] // 256, flip, 0)
    doc_col[...] = jnp.broadcast_to(doc_row[...], (length, length)).T
    ag_step(0, 2)
    ag_step(3, 0)
    ag_step(1, 1)
    go_step(2)
    ag_step(2, 0)
    go_spread(0)
    go_spread(1)
    ag_step(0, 3)
    ag_step(3, 1)
    go_step(3)
    go_spread(2)
    ag_step(1, 2)
    ag_step(2, 1)
    go_step(4)
    go_spread(3)
    go_spread(4)
    ag_step(3, 2)
    ag_step(1, 3)
    ag_step(2, 2)
    ag_step(3, 3)
    ag_step(2, 3)
    ag_end()

    cosine, sine = cos_in[...], sin_in[...]
    scale = 1.0 / math.sqrt(HD)

    def project():
        joined[...] = dot(tok[...], wq[...]).astype(BF16)

    def attend(h):
        cols = slice(h * HD, (h + 1) * HD)
        width = 2 * HD
        qr = turned(joined[:, h * HD:(h + 1) * HD].astype(F32), cosine, sine)
        kr = turned(joined[:, width + h * HD:width + (h + 1) * HD].astype(F32), cosine, sine)
        q_rot[h] = qr
        k_rot[h] = kr
        scores = lax.dot_general(qr, kr, NT, precision=HIGHEST, preferred_element_type=F32) * scale
        row = lax.broadcasted_iota(jnp.int32, (length, length), 0)
        col = lax.broadcasted_iota(jnp.int32, (length, length), 1)
        allowed = (col <= row) & (doc_row[...] == doc_col[...])
        scores = jnp.where(allowed, scores, -1e30)
        expo = jnp.exp(scores - jnp.max(scores, axis=1, keepdims=True))
        p = expo / jnp.sum(expo, axis=1, keepdims=True)
        probs[h] = p
        values = joined[:, 2 * width + h * HD:2 * width + (h + 1) * HD]
        ctx[:, cols] = dot(p.astype(BF16), values).astype(BF16)

    def retreat(h):
        width = 2 * HD
        p = probs[h]
        d_out = back[:, h * HD:(h + 1) * HD]
        values = joined[:, 2 * width + h * HD:2 * width + (h + 1) * HD]
        d_val = jnp.dot(p.T, d_out.astype(F32), precision=HIGHEST, preferred_element_type=F32)
        d_p = dot_nt(d_out, values)
        d_s = p * (d_p - jnp.sum(p * d_p, axis=1, keepdims=True)) * scale
        d_q = jnp.dot(d_s, k_rot[h], precision=HIGHEST, preferred_element_type=F32)
        d_k = jnp.dot(d_s.T, q_rot[h], precision=HIGHEST, preferred_element_type=F32)
        grad_j[:, h * HD:(h + 1) * HD] = turned(d_q, cosine, -sine).astype(BF16)
        grad_j[:, width + h * HD:width + (h + 1) * HD] = turned(d_k, cosine, -sine).astype(BF16)
        grad_j[:, 2 * width + h * HD:2 * width + (h + 1) * HD] = d_val.astype(BF16)

    def rs_y(way, d, j):
        return remote(
            sq.at[way, d - 1, j], rq.at[way, d - 1, j], rs_ss.at[way, d - 1, j], rs_rs.at[way, d - 1, j],
            up if way == 0 else down,
        )

    def rs_step(j, u):
        d = 4 - u
        for way in (0, 1):
            if d == 4 and not long(way, j):
                continue
            sign = 1 if way == 0 else -1
            own = grad_q[row_at((zh - j + NZ) % NZ, (y + sign * d + NY) % NY), :]
            if d < 3 or (d == 3 and long(way, j)):
                rs_y(way, d + 1, j).wait_recv()
                own = own + rq[way, d, j].astype(F32)
            sq[way, d - 1, j] = own.astype(BF16)
            rs_y(way, d, j).start()

    def rs_here(j):
        for way in (0, 1):
            rs_y(way, 1, j).wait_recv()
        own = grad_q[row_at((zh - j + NZ) % NZ, y), :]
        return own + rq[0, 0, j].astype(F32) + rq[1, 0, j].astype(F32)

    def rs_z(j):
        return remote(zsq.at[j], zrq.at[j], rsz_ss.at[j], rsz_rs.at[j], at_z(NZ - j))

    def rs_out(j):
        zsq[j] = rs_here(j).astype(BF16)
        rs_z(j).start()

    def rs_end():
        total = rs_here(0)
        for j in (1, 2, 3):
            rs_z(j).wait_recv()
            total = total + zrq[j].astype(F32)
        for c in range(3):
            gq_out[c] = total[:, c * third:(c + 1) * third]

    def rs_drain():
        for j in range(NZ):
            if j > 0:
                rs_z(j).wait_send()
            for way in (0, 1):
                for d in (1, 2, 3, 4):
                    if d < 4 or long(way, j):
                        rs_y(way, d, j).wait_send()

    def gr_z(r, k):
        return remote(zso.at[r, k], zro.at[r, k], grz_ss.at[r, k], grz_rs.at[r, k], at_z(k))

    def gr_spread(r):
        for k in (1, 3, 2):
            zso[r, k] = grad_o[row_at((zh + k) % NZ, (y + r) % NY), :].astype(BF16)
            gr_z(r, k).start()

    def gr_own(r):
        total = grad_o[row_at(zh, (y + r) % NY), :]
        for k in (1, 2, 3):
            gr_z(r, k).wait_recv()
            total = total + zro[r, k].astype(F32)
        return total

    def gr_y(way, d):
        return remote(
            so.at[way, d - 1], ro.at[way, d - 1], gr_ss.at[way, d - 1], gr_rs.at[way, d - 1],
            up if way == 0 else down,
        )

    def gr_step(u):
        d = 4 - u
        for way in (0, 1):
            if d == 4 and way == 1:
                continue
            own = gr_own(d if way == 0 else NY - d)
            if d < 3 or (d == 3 and way == 0):
                gr_y(way, d + 1).wait_recv()
                own = own + ro[way, d].astype(F32)
            so[way, d - 1] = own.astype(BF16)
            gr_y(way, d).start()

    def gr_end():
        total = gr_own(0)
        for way in (0, 1):
            gr_y(way, 1).wait_recv()
            total = total + ro[way, 0].astype(F32)
        go_out[...] = total

    def gr_drain():
        for way in (0, 1):
            for d in (1, 2, 3, 4):
                if d < 4 or way == 0:
                    gr_y(way, d).wait_send()

        def body(r, c):
            for k in (1, 2, 3):
                gr_z(r, k).wait_send()
            return c

        lax.fori_loop(0, NY, body, 0)

    half = length // NC
    quarter = half // NX
    eighth = quarter // NL
    half_at = pl.ds(pl.multiple_of(core * half, 16), half)
    quarter_at = pl.ds(pl.multiple_of(core * half + x * quarter, 16), quarter)
    eighth_at = pl.ds(pl.multiple_of(core * half + x * quarter + lo * eighth, 16), eighth)

    def mx_core():
        away = pl.ds(pl.multiple_of((1 - core) * half, 16), half)
        return remote(part.at[away, :], part_c, mx_ss.at[0], mx_rs.at[0], core_peer)

    def mx_x(k):
        away = pl.ds(pl.multiple_of(((x + k) % NX) * quarter, 16), quarter)
        return remote(sum_c.at[away, :], recv_x.at[k - 1], mx_ss.at[k], mx_rs.at[k], at_x(k))

    def mx_lo():
        away = pl.ds(pl.multiple_of((1 - lo) * eighth, 16), eighth)
        return remote(sum_x.at[away, :], recv_l, mx_ss.at[4], mx_rs.at[4], lo_peer)

    def back_lo(got=False):
        at = eighth_at
        if got:
            at = pl.ds(pl.multiple_of(core * half + x * quarter + (1 - lo) * eighth, 16), eighth)
        return remote(mixed.at[at, :], mixed.at[at, :], mx_ss.at[5], mx_rs.at[5], lo_peer)

    def back_x(k, got=False):
        at = quarter_at
        if got:
            at = pl.ds(pl.multiple_of(core * half + ((x - k + NX) % NX) * quarter, 16), quarter)
        return remote(mixed.at[at, :], mixed.at[at, :], mx_ss.at[5 + k], mx_rs.at[5 + k], at_x(k))

    def back_core(got=False):
        at = half_at
        if got:
            at = pl.ds(pl.multiple_of((1 - core) * half, 16), half)
        return remote(mixed.at[at, :], mixed.at[at, :], mx_ss.at[9], mx_rs.at[9], core_peer)

    def stage_x():
        mx_core().wait_recv()

        def body(i, c):
            r = pl.ds(pl.multiple_of(i * 16, 16), 16)
            there = pl.ds(pl.multiple_of(core * half + i * 16, 16), 16)
            sum_c[r, :] = (part[there, :].astype(F32) + part_c[r, :].astype(F32)).astype(BF16)
            return c

        lax.fori_loop(0, half // 16, body, 0)
        for k in (1, 2, 3):
            mx_x(k).start()

    def stage_lo():
        total = sum_c[pl.ds(pl.multiple_of(x * quarter, 16), quarter), :].astype(F32)
        for k in (1, 2, 3):
            mx_x(k).wait_recv()
            total = total + recv_x[k - 1].astype(F32)
        sum_x[...] = total.astype(BF16)
        mx_lo().start()

    def stage_back():
        mx_lo().wait_recv()
        own = sum_x[pl.ds(pl.multiple_of(lo * eighth, 16), eighth), :].astype(F32)
        total = tok[eighth_at, :].astype(F32) + (own + recv_l[...].astype(F32))
        mixed[eighth_at, :] = total.astype(BF16)
        back_lo().start()

    def stage_back_x():
        back_lo(True).wait_recv()
        for k in (1, 2, 3):
            back_x(k).start()

    def stage_back_core():
        for k in (1, 2, 3):
            back_x(k, True).wait_recv()
        back_core().start()

    def widen(i, c):
        r = pl.ds(pl.multiple_of(i * 512, 512), 512)
        grad_o[r, :] = dot(cot_t[r, :], ctx[...])
        return c

    def widen_q(i, c):
        r = pl.ds(pl.multiple_of(i * 512, 512), 512)
        grad_q[r, :] = dot(tok_t[r, :], grad_j[...])
        return c

    def outward(i, c):
        r = pl.ds(pl.multiple_of(i * 512, 512), 512)
        part[:, r] = dot_nt(ctx[...], wo[r, :]).astype(BF16)
        return c

    def leave(got):
        at = half_at
        if got:
            at = pl.ds(pl.multiple_of((1 - core) * half, 16), half)
        return pltpu.make_async_copy(mixed.at[at, :], mixed_out.at[at, :], load_sem.at[got])

    chunks = tok.shape[1] // 512
    project()
    attend(0)
    attend(1)
    lax.fori_loop(0, chunks, widen, 0)
    for r in (4, 3, 5, 2, 6, 1, 7, 0):
        gr_spread(r)
    go_end()
    lax.fori_loop(0, chunks, outward, 0)
    mx_core().start()
    back[...] = dot(cot[...], wo[...]).astype(BF16)
    retreat(0)
    retreat(1)
    lax.fori_loop(0, chunks, widen_q, 0)
    rs_step(2, 0)
    rs_step(1, 0)
    stage_x()
    rs_step(2, 1)
    rs_step(3, 0)
    gr_step(0)
    rs_step(1, 1)
    rs_step(2, 2)
    rs_step(0, 0)
    gr_step(1)
    stage_lo()
    rs_step(3, 1)
    rs_step(1, 2)
    rs_step(2, 3)
    stage_back()
    rs_step(0, 1)
    gr_step(2)
    rs_step(3, 2)
    rs_out(2)
    rs_step(1, 3)
    stage_back_x()
    rs_step(0, 2)
    rs_step(3, 3)
    rs_out(1)
    gr_step(3)
    rs_step(0, 3)
    rs_out(3)
    stage_back_core()
    leave(0).start()
    gr_end()
    back_core(True).wait_recv()
    leave(1).start()
    rs_end()

    leave(0).wait()
    leave(1).wait()
    ag_drain()
    go_drain()
    rs_drain()
    gr_drain()
    mx_core().wait_send()
    mx_lo().wait_send()
    back_lo().wait_send()
    back_core().wait_send()
    for k in (1, 2, 3):
        mx_x(k).wait_send()
        back_x(k).wait_send()


def local(tokens, doc_ids, qkv_weight, out_weight, cotangent):
    length, width = tokens.shape
    rows, _, feature = qkv_weight.shape
    joined_width = 3 * feature
    heads = feature // HD
    frequency = 10000.0 ** (-2.0 * np.arange(HD // 2) / HD)
    angles = np.arange(length)[:, None] * frequency[None, :]
    cosine = jnp.asarray(np.concatenate([np.cos(angles), np.cos(angles)], axis=1), F32)
    sine = jnp.asarray(np.concatenate([-np.sin(angles), np.sin(angles)], axis=1), F32)
    vmem = pl.BlockSpec(memory_space=pltpu.VMEM)
    hbm = pl.BlockSpec(memory_space=pl.ANY)
    dma = pltpu.SemaphoreType.DMA
    half = length // NC
    mixed, grad_q, grad_o = pl.pallas_call(
        kernel,
        out_shape=(
            jax.ShapeDtypeStruct((length, width), BF16),
            jax.ShapeDtypeStruct((3, rows, feature), F32),
            jax.ShapeDtypeStruct((rows, feature), F32),
        ),
        in_specs=[hbm, hbm] + [vmem] * 5,
        out_specs=(hbm, vmem, vmem),
        scratch_shapes=[
            pltpu.VMEM((length, width), BF16),
            pltpu.VMEM((length, width), BF16),
            pltpu.VMEM((width, length), BF16),
            pltpu.VMEM((width, length), BF16),
            pltpu.VMEM((width, joined_width), BF16),
            pltpu.VMEM((width, feature), BF16),
            pltpu.VMEM((length, joined_width), BF16),
            pltpu.VMEM((length, feature), BF16),
            pltpu.VMEM((length, feature), BF16),
            pltpu.VMEM((heads, length, length), F32),
            pltpu.VMEM((heads, length, HD), F32),
            pltpu.VMEM((heads, length, HD), F32),
            pltpu.VMEM((length, joined_width), BF16),
            pltpu.VMEM((width, joined_width), F32),
            pltpu.VMEM((width, feature), F32),
            pltpu.VMEM((2, 4, NZ, rows, joined_width), BF16),
            pltpu.VMEM((2, 4, NZ, rows, joined_width), BF16),
            pltpu.VMEM((2, 4, rows, feature), BF16),
            pltpu.VMEM((2, 4, rows, feature), BF16),
            pltpu.VMEM((NZ, rows, joined_width), BF16),
            pltpu.VMEM((NZ, rows, joined_width), BF16),
            pltpu.VMEM((NY, NZ, rows, feature), BF16),
            pltpu.VMEM((NY, NZ, rows, feature), BF16),
            pltpu.VMEM((length, length), jnp.int32),
            pltpu.VMEM((length, width), BF16),
            pltpu.VMEM((half, width), BF16),
            pltpu.VMEM((half, width), BF16),
            pltpu.VMEM((NX - 1, half // NX, width), BF16),
            pltpu.VMEM((half // NX, width), BF16),
            pltpu.VMEM((half // NX // NL, width), BF16),
            pltpu.VMEM((length, width), BF16),
            dma((2,)),
            dma((2, 4, NZ)),
            dma((2, 4, NZ)),
            dma((NZ,)),
            dma((NZ,)),
            dma((2, 4, NZ)),
            dma((2, 4, NZ)),
            dma((NZ,)),
            dma((NZ,)),
            dma((2, 4)),
            dma((2, 4)),
            dma((NY, NZ)),
            dma((NY, NZ)),
            dma((2, 4)),
            dma((2, 4)),
            dma((NY, NZ)),
            dma((NY, NZ)),
            dma((10,)),
            dma((10,)),
        ],
        compiler_params=pltpu.CompilerParams(
            collective_id=0, has_side_effects=True, vmem_limit_bytes=56 * 1024 * 1024
        ),
        name="layer",
    )(
        tokens,
        cotangent,
        qkv_weight.transpose(1, 0, 2),
        out_weight.T,
        doc_ids.reshape(1, length),
        cosine,
        sine,
    )
    return mixed, grad_q.transpose(1, 0, 2), grad_o.T


def solution(mesh):
    placed = (
        P("blk", None),
        P("blk"),
        P("blk", None, "tensor"),
        P("tensor", "blk"),
        P("blk", None),
    )
    return jax.shard_map(
        local,
        mesh=mesh,
        in_specs=placed,
        out_specs=(P("blk", None), P("blk", None, "tensor"), P("tensor", "blk")),
        check_vma=False,
    )
```

```python
import math

import jax
import jax.numpy as jnp
import numpy as np
from jax import lax
from jax.experimental import pallas as pl
from jax.experimental.pallas import tpu as pltpu
from jax.sharding import PartitionSpec as P

HD = 128
NZ, NY = 4, 8
NX, NL, NC = 4, 2, 2
F32 = jnp.float32
BF16 = jnp.bfloat16
HIGHEST = lax.Precision.HIGHEST
NT = (((1,), (1,)), ((), ()))


def dot(a, b):
    return jnp.dot(a, b, preferred_element_type=F32)


def dot_nt(a, b):
    return lax.dot_general(a, b, NT, preferred_element_type=F32)


def turned(x, cosine, sine):
    half = x.shape[1] // 2
    swapped = jnp.concatenate([x[:, half:], x[:, :half]], axis=1)
    return x * cosine + swapped * sine


def kernel(
    tokens_hbm, cot_hbm, wq_in, wo_in, doc_in, cos_in, sin_in,
    mixed_out, gq_out, go_out,
    tok, cot, tok_t, cot_t, docs, staged, w, joined, ctx, back, probs, q_rot, k_rot, grad_j,
    grad, sq, rq, zs, zr, part, part_c, sum_c, recv_x, sum_x, recv_z, mixed,
    load_sem, ag_ss, ag_rs, agz_ss, agz_rs, rs_ss, rs_rs, rsz_ss, rsz_rs, tk_ss, tk_rs, mx_ss, mx_rs,
):
    blk = lax.axis_index("blk")
    ten = lax.axis_index("tensor")
    zh, y = blk // NY, blk % NY
    x, rest = ten // (NL * NC), ten % (NL * NC)
    lo, core = rest // NC, rest % NC
    rows = wq_in.shape[1]
    length = tok.shape[1]
    width = tok.shape[2]
    pick = zh % 2

    def at_z(k):
        return (((zh + k) % NZ) * NY + y, ten)

    def at_y(step):
        return (zh * NY + (y + step + NY) % NY, ten)

    def at_x(k):
        return (blk, ((x + k) % NX) * (NL * NC) + rest)

    up, down = at_y(1), at_y(-1)
    core_peer = (blk, ten + 1 - 2 * core)
    other_lo = ten + NC - 2 * NC * lo
    lo_peer = (blk, other_lo)
    other_blk = blk + NY - 2 * NY * pick
    partner = (other_blk, ten)
    partner_lo = (other_blk, other_lo)

    load_tok = pltpu.make_async_copy(tokens_hbm, tok.at[0], load_sem.at[0])
    load_cot = pltpu.make_async_copy(cot_hbm, cot.at[0], load_sem.at[1])
    load_tok.start()
    load_cot.start()

    barrier = pltpu.get_barrier_semaphore()
    peers = [at_z(k) for k in (1, 2, 3)] + [at_x(k) for k in (1, 2, 3)]
    peers += [up, down, core_peer, lo_peer, partner_lo]
    for peer in peers:
        pl.semaphore_signal(barrier, inc=1, device_id=peer, device_id_type=pl.DeviceIdType.MESH)

    def row_at(z, yy):
        return pl.ds(pl.multiple_of((z * NY + yy) * rows, 16), rows)

    for h in range(2):
        for c in range(3):
            staged[h, :, c * HD:(c + 1) * HD] = wq_in[c, :, h * HD:(h + 1) * HD]
        staged[h, :, 3 * HD:] = wo_in[:, h * HD:(h + 1) * HD]
    mine = row_at(zh, y)
    w[mine, :] = staged[pick]
    docs[0] = jnp.broadcast_to(doc_in[...], docs.shape[1:])
    load_tok.wait()
    load_cot.wait()
    pl.semaphore_wait(barrier, len(peers))

    def remote(src, dst, ss, rs, peer):
        return pltpu.make_async_remote_copy(
            src_ref=src, dst_ref=dst, send_sem=ss, recv_sem=rs,
            device_id=peer, device_id_type=pl.DeviceIdType.MESH,
        )

    def long(way, j):
        return j % 2 == way

    half = length // NC
    quarter = half // NX
    eighth = quarter // NL

    def place(c, xx=None, ll=None):
        if xx is None:
            return pl.ds(pl.multiple_of(c * half, 16), half)
        if ll is None:
            return pl.ds(pl.multiple_of(c * half + xx * quarter, 16), quarter)
        return pl.ds(pl.multiple_of(c * half + xx * quarter + ll * eighth, 16), eighth)

    def tk_copy(i, stage, got=False):
        a = (tok, cot)[i]
        if stage == 0:
            at = place(core, x, lo)
            return remote(a.at[0, at, :], a.at[1, at, :], tk_ss.at[i, 0], tk_rs.at[i, 0], partner)
        if stage == 1:
            at, peer = place(core, x, 1 - lo if got else lo), lo_peer
        elif stage == 5:
            at, peer = place(1 - core if got else core), core_peer
        else:
            k = stage - 1
            at, peer = place(core, (x - k + NX) % NX if got else x), at_x(k)
        return remote(a.at[1, at, :], a.at[1, at, :], tk_ss.at[i, stage], tk_rs.at[i, stage], peer)

    def tk_lo(i):
        tk_copy(i, 0).wait_recv()
        tk_copy(i, 1).start()

    def tk_x(i):
        tk_copy(i, 1, True).wait_recv()
        for stage in (2, 4, 3):
            tk_copy(i, stage).start()

    def tk_core(i):
        for stage in (2, 4, 3):
            tk_copy(i, stage, True).wait_recv()
        tk_copy(i, 5).start()

    def tk_end(i):
        tk_copy(i, 5, True).wait_recv()

    def tk_drain():
        for i in (0, 1):
            for stage in range(6):
                tk_copy(i, stage).wait_send()

    def doc_copy():
        return remote(docs.at[0], docs.at[1], tk_ss.at[0, 6], tk_rs.at[0, 6], partner)

    def ag_z(k):
        return remote(
            staged.at[(zh + k) % 2], w.at[mine, :], agz_ss.at[k], agz_rs.at[k], at_z(k)
        )

    def ag_y(way, s, j, got):
        sign = 1 if way == 0 else -1
        off = s + 1 if got else s
        here = row_at((zh - j + NZ) % NZ, (y - sign * off + 2 * NY) % NY)
        return remote(
            w.at[here, :], w.at[here, :], ag_ss.at[way, s, j], ag_rs.at[way, s, j],
            up if way == 0 else down,
        )

    def ag_step(j, s):
        if s == 0 and j > 0:
            here = row_at((zh - j + NZ) % NZ, y)
            remote(w.at[here, :], w.at[here, :], agz_ss.at[j], agz_rs.at[j], at_z(j)).wait_recv()
        for way in (0, 1):
            if s > 0:
                ag_y(way, s - 1, j, True).wait_recv()
            if s < 3 or long(way, j):
                ag_y(way, s, j, False).start()

    def ag_end():
        for j in range(NZ):
            for way in (0, 1):
                if long(way, j):
                    ag_y(way, 3, j, True).wait_recv()

    def ag_drain():
        for k in (1, 2, 3):
            ag_z(k).wait_send()
        for j in range(NZ):
            for way in (0, 1):
                for s in range(4):
                    if s < 3 or long(way, j):
                        ag_y(way, s, j, False).wait_send()

    def flip(a, a_t, m):
        def body(i, c):
            cols = pl.ds(pl.multiple_of(i * 256, 256), 256)
            a_t[cols, m * length:(m + 1) * length] = a[m, :, cols].T
            return c

        lax.fori_loop(0, width // 256, body, 0)

    cosine, sine = cos_in[...], sin_in[...]
    scale = 1.0 / math.sqrt(HD)

    def rows_of(m):
        return slice(m * length, (m + 1) * length)

    def project(m):
        joined[rows_of(m), :] = dot(tok[m], w[:, :3 * HD]).astype(BF16)

    def attend(m):
        qr = turned(joined[rows_of(m), :HD].astype(F32), cosine, sine)
        kr = turned(joined[rows_of(m), HD:2 * HD].astype(F32), cosine, sine)
        q_rot[m] = qr
        k_rot[m] = kr
        scores = lax.dot_general(qr, kr, NT, precision=HIGHEST, preferred_element_type=F32) * scale
        row = lax.broadcasted_iota(jnp.int32, (length, length), 0)
        col = lax.broadcasted_iota(jnp.int32, (length, length), 1)
        ids = jnp.broadcast_to(docs[m, :1, :], (length, length))
        allowed = (col <= row) & (ids == ids.T)
        scores = jnp.where(allowed, scores, -1e30)
        expo = jnp.exp(scores - jnp.max(scores, axis=1, keepdims=True))
        p = expo / jnp.sum(expo, axis=1, keepdims=True)
        probs[m] = p
        ctx[rows_of(m), :] = dot(p.astype(BF16), joined[rows_of(m), 2 * HD:]).astype(BF16)

    def retreat(m):
        p = probs[m]
        d_out = back[rows_of(m), :]
        d_val = jnp.dot(p.T, d_out.astype(F32), precision=HIGHEST, preferred_element_type=F32)
        d_p = dot_nt(d_out, joined[rows_of(m), 2 * HD:])
        d_s = p * (d_p - jnp.sum(p * d_p, axis=1, keepdims=True)) * scale
        d_q = jnp.dot(d_s, k_rot[m], precision=HIGHEST, preferred_element_type=F32)
        d_k = jnp.dot(d_s.T, q_rot[m], precision=HIGHEST, preferred_element_type=F32)
        grad_j[rows_of(m), :HD] = turned(d_q, cosine, -sine).astype(BF16)
        grad_j[rows_of(m), HD:2 * HD] = turned(d_k, cosine, -sine).astype(BF16)
        grad_j[rows_of(m), 2 * HD:] = d_val.astype(BF16)

    chunks = width // 512

    def outward(m):
        def body(i, c):
            r = pl.ds(pl.multiple_of(i * 512, 512), 512)
            part[m, :, r] = dot_nt(ctx[rows_of(m), :], w[r, 3 * HD:]).astype(BF16)
            return c

        lax.fori_loop(0, chunks, body, 0)

    def widen_o():
        def body(i, c):
            r = pl.ds(pl.multiple_of(i * 512, 512), 512)
            grad[r, 3 * HD:] = dot(cot_t[r, :], ctx[...])
            return c

        lax.fori_loop(0, chunks, body, 0)

    def widen_q():
        def body(i, c):
            r = pl.ds(pl.multiple_of(i * 512, 512), 512)
            grad[r, :3 * HD] = dot(tok_t[r, :], grad_j[...])
            return c

        lax.fori_loop(0, chunks, body, 0)

    def retract():
        for m in (0, 1):
            back[rows_of(m), :] = dot(cot[m], w[:, 3 * HD:]).astype(BF16)

    def rs_y(way, d, j):
        return remote(
            sq.at[way, d - 1, j], rq.at[way, d - 1, j], rs_ss.at[way, d - 1, j], rs_rs.at[way, d - 1, j],
            up if way == 0 else down,
        )

    def rs_step(j, u):
        d = 4 - u
        for way in (0, 1):
            if d == 4 and not long(way, j):
                continue
            sign = 1 if way == 0 else -1
            own = grad[row_at((zh - j + NZ) % NZ, (y + sign * d + NY) % NY), :]
            if d < 3 or (d == 3 and long(way, j)):
                rs_y(way, d + 1, j).wait_recv()
                own = own + rq[way, d, j].astype(F32)
            sq[way, d - 1, j] = own.astype(BF16)
            rs_y(way, d, j).start()

    def rs_here(j):
        for way in (0, 1):
            rs_y(way, 1, j).wait_recv()
        own = grad[row_at((zh - j + NZ) % NZ, y), :]
        return own + rq[0, 0, j].astype(F32) + rq[1, 0, j].astype(F32)

    def rs_z(j):
        return remote(zs.at[j], zr.at[j], rsz_ss.at[j], rsz_rs.at[j], at_z(NZ - j))

    def rs_out(j):
        zs[j] = rs_here(j).astype(BF16)
        rs_z(j).start()

    def rs_end():
        total = rs_here(0)
        for j in (1, 2, 3):
            rs_z(j).wait_recv()
        total = total + zr[2].astype(F32)
        across = zr[1].astype(F32) + zr[3].astype(F32)
        for at, value in ((pick, total), (1 - pick, across)):
            cols = pl.ds(pl.multiple_of(at * HD, HD), HD)
            for c in range(3):
                gq_out[c, :, cols] = value[:, c * HD:(c + 1) * HD]
            go_out[:, cols] = value[:, 3 * HD:]

    def rs_drain():
        for j in range(NZ):
            if j > 0:
                rs_z(j).wait_send()
            for way in (0, 1):
                for d in (1, 2, 3, 4):
                    if d < 4 or long(way, j):
                        rs_y(way, d, j).wait_send()

    def mx_core(m):
        return remote(part.at[m, place(1 - core), :], part_c.at[m], mx_ss.at[m, 0], mx_rs.at[m, 0], core_peer)

    def mx_x(m, k):
        away = pl.ds(pl.multiple_of(((x + k) % NX) * quarter, 16), quarter)
        return remote(sum_c.at[m, away, :], recv_x.at[m, k - 1], mx_ss.at[m, k], mx_rs.at[m, k], at_x(k))

    def mx_z(i):
        m, peer = ((0, lo_peer), (1, partner), (1, partner_lo))[i]
        at = pl.ds(pl.multiple_of((lo if i == 1 else 1 - lo) * eighth, 16), eighth)
        return remote(sum_x.at[m, at, :], recv_z.at[i], mx_ss.at[0, 4 + i], mx_rs.at[0, 4 + i], peer)

    def back_copy(stage, got=False):
        if stage == 0:
            at, peer = place(core, x, 1 - lo if got else lo), lo_peer
        elif stage == 4:
            at, peer = place(1 - core if got else core), core_peer
        else:
            at, peer = place(core, (x - stage + NX) % NX if got else x), at_x(stage)
        return remote(mixed.at[at, :], mixed.at[at, :], mx_ss.at[1, 4 + stage], mx_rs.at[1, 4 + stage], peer)

    def stage_x(m):
        mx_core(m).wait_recv()

        def body(i, c):
            r = pl.ds(pl.multiple_of(i * 16, 16), 16)
            there = pl.ds(pl.multiple_of(core * half + i * 16, 16), 16)
            sum_c[m, r, :] = (part[m, there, :].astype(F32) + part_c[m, r, :].astype(F32)).astype(BF16)
            return c

        lax.fori_loop(0, half // 16, body, 0)
        for k in (1, 3, 2):
            mx_x(m, k).start()

    def stage_z(m):
        total = sum_c[m, pl.ds(pl.multiple_of(x * quarter, 16), quarter), :].astype(F32)
        for k in (1, 3, 2):
            mx_x(m, k).wait_recv()
            total = total + recv_x[m, k - 1].astype(F32)
        sum_x[m] = total.astype(BF16)
        for i in ((0,), (1, 2))[m]:
            mx_z(i).start()

    def stage_back():
        total = sum_x[0, pl.ds(pl.multiple_of(lo * eighth, 16), eighth), :].astype(F32)
        for i in range(3):
            mx_z(i).wait_recv()
            total = total + recv_z[i].astype(F32)
        at = place(core, x, lo)
        mixed[at, :] = (tok[0, at, :].astype(F32) + total).astype(BF16)
        back_copy(0).start()

    def stage_back_x():
        back_copy(0, True).wait_recv()
        for k in (1, 3, 2):
            back_copy(k).start()

    def stage_back_core():
        for k in (1, 3, 2):
            back_copy(k, True).wait_recv()
        back_copy(4).start()

    def mx_drain():
        for m in (0, 1):
            mx_core(m).wait_send()
            for k in (1, 2, 3):
                mx_x(m, k).wait_send()
        for i in range(3):
            mx_z(i).wait_send()
        for stage in range(5):
            back_copy(stage).wait_send()

    def leave(got):
        at = place(1 - core if got else core)
        return pltpu.make_async_copy(mixed.at[at, :], mixed_out.at[at, :], load_sem.at[got])

    tk_copy(0, 0).start()
    ag_step(0, 0)
    ag_z(1).start()
    ag_z(3).start()
    tk_copy(1, 0).start()
    doc_copy().start()
    ag_z(2).start()
    flip(tok, tok_t, 0)
    ag_step(0, 1)
    tk_lo(0)
    ag_step(1, 0)
    ag_step(3, 0)
    flip(cot, cot_t, 0)
    ag_step(0, 2)
    ag_step(1, 1)
    tk_x(0)
    tk_lo(1)
    ag_step(2, 0)
    ag_step(3, 1)
    ag_step(0, 3)
    ag_step(1, 2)
    tk_x(1)
    ag_step(2, 1)
    ag_step(3, 2)
    ag_step(1, 3)
    tk_core(0)
    ag_step(2, 2)
    ag_step(3, 3)
    ag_step(2, 3)
    tk_end(0)
    flip(tok, tok_t, 1)
    ag_end()

    project(0)
    attend(0)
    tk_core(1)
    outward(0)
    mx_core(0).start()
    project(1)
    doc_copy().wait_recv()
    attend(1)
    outward(1)
    mx_core(1).start()
    tk_end(1)
    stage_x(0)
    flip(cot, cot_t, 1)
    stage_x(1)
    retract()
    retreat(0)
    retreat(1)
    stage_z(0)
    widen_o()
    widen_q()
    rs_step(2, 0)
    rs_step(1, 0)
    stage_z(1)
    rs_step(2, 1)
    rs_step(3, 0)
    rs_step(1, 1)
    rs_step(2, 2)
    rs_step(0, 0)
    rs_step(3, 1)
    stage_back()
    rs_step(1, 2)
    rs_step(2, 3)
    rs_step(0, 1)
    stage_back_x()
    rs_step(3, 2)
    rs_out(2)
    rs_step(1, 3)
    rs_step(0, 2)
    rs_step(3, 3)
    rs_out(1)
    rs_step(0, 3)
    rs_out(3)
    stage_back_core()
    leave(0).start()
    rs_end()
    back_copy(4, True).wait_recv()
    leave(1).start()

    ag_drain()
    tk_drain()
    doc_copy().wait_send()
    rs_drain()
    mx_drain()
    leave(0).wait()
    leave(1).wait()


def local(tokens, doc_ids, qkv_weight, out_weight, cotangent):
    length, width = tokens.shape
    rows, _, feature = qkv_weight.shape
    block = 4 * HD
    frequency = 10000.0 ** (-2.0 * np.arange(HD // 2) / HD)
    angles = np.arange(length)[:, None] * frequency[None, :]
    cosine = jnp.asarray(np.concatenate([np.cos(angles), np.cos(angles)], axis=1), F32)
    sine = jnp.asarray(np.concatenate([-np.sin(angles), np.sin(angles)], axis=1), F32)
    vmem = pl.BlockSpec(memory_space=pltpu.VMEM)
    hbm = pl.BlockSpec(memory_space=pl.ANY)
    dma = pltpu.SemaphoreType.DMA
    half = length // NC
    quarter = half // NX
    mixed, grad_q, grad_o = pl.pallas_call(
        kernel,
        out_shape=(
            jax.ShapeDtypeStruct((length, width), BF16),
            jax.ShapeDtypeStruct((3, rows, feature), F32),
            jax.ShapeDtypeStruct((rows, feature), F32),
        ),
        in_specs=[hbm, hbm] + [vmem] * 5,
        out_specs=(hbm, vmem, vmem),
        scratch_shapes=[
            pltpu.VMEM((2, length, width), BF16),
            pltpu.VMEM((2, length, width), BF16),
            pltpu.VMEM((width, 2 * length), BF16),
            pltpu.VMEM((width, 2 * length), BF16),
            pltpu.VMEM((2, 8, length), jnp.int32),
            pltpu.VMEM((2, rows, block), BF16),
            pltpu.VMEM((width, block), BF16),
            pltpu.VMEM((2 * length, 3 * HD), BF16),
            pltpu.VMEM((2 * length, HD), BF16),
            pltpu.VMEM((2 * length, HD), BF16),
            pltpu.VMEM((2, length, length), F32),
            pltpu.VMEM((2, length, HD), F32),
            pltpu.VMEM((2, length, HD), F32),
            pltpu.VMEM((2 * length, 3 * HD), BF16),
            pltpu.VMEM((width, block), F32),
            pltpu.VMEM((2, 4, NZ, rows, block), BF16),
            pltpu.VMEM((2, 4, NZ, rows, block), BF16),
            pltpu.VMEM((NZ, rows, block), BF16),
            pltpu.VMEM((NZ, rows, block), BF16),
            pltpu.VMEM((2, length, width), BF16),
            pltpu.VMEM((2, half, width), BF16),
            pltpu.VMEM((2, half, width), BF16),
            pltpu.VMEM((2, NX - 1, quarter, width), BF16),
            pltpu.VMEM((2, quarter, width), BF16),
            pltpu.VMEM((3, quarter // NL, width), BF16),
            pltpu.VMEM((length, width), BF16),
            dma((2,)),
            dma((2, 4, NZ)),
            dma((2, 4, NZ)),
            dma((NZ,)),
            dma((NZ,)),
            dma((2, 4, NZ)),
            dma((2, 4, NZ)),
            dma((NZ,)),
            dma((NZ,)),
            dma((2, 7)),
            dma((2, 7)),
            dma((2, 9)),
            dma((2, 9)),
        ],
        compiler_params=pltpu.CompilerParams(
            collective_id=0, has_side_effects=True, vmem_limit_bytes=56 * 1024 * 1024
        ),
        name="layer",
    )(
        tokens,
        cotangent,
        qkv_weight.transpose(1, 0, 2),
        out_weight.T,
        doc_ids.reshape(1, length),
        cosine,
        sine,
    )
    return mixed, grad_q.transpose(1, 0, 2), grad_o.T


def solution(mesh):
    placed = (
        P("blk", None),
        P("blk"),
        P("blk", None, "tensor"),
        P("tensor", "blk"),
        P("blk", None),
    )
    return jax.shard_map(
        local,
        mesh=mesh,
        in_specs=placed,
        out_specs=(P("blk", None), P("blk", None, "tensor"), P("tensor", "blk")),
        check_vma=False,
    )
```

```python
import math

import jax
import jax.numpy as jnp
import numpy as np
from jax import lax
from jax.experimental import pallas as pl
from jax.experimental.pallas import tpu as pltpu
from jax.sharding import PartitionSpec as P

HD = 128
NZ, NY = 4, 8
NX, NL, NC = 4, 2, 2
F32 = jnp.float32
BF16 = jnp.bfloat16
HIGHEST = lax.Precision.HIGHEST
NT = (((1,), (1,)), ((), ()))


def dot(a, b):
    return jnp.dot(a, b, preferred_element_type=F32)


def dot_nt(a, b):
    return lax.dot_general(a, b, NT, preferred_element_type=F32)


def turned(x, cosine, sine):
    half = x.shape[1] // 2
    swapped = jnp.concatenate([x[:, half:], x[:, :half]], axis=1)
    return x * cosine + swapped * sine


def kernel(
    tokens_hbm, cot_hbm, wq_in, wo_in, doc_in, cos_in, sin_in,
    mixed_out, gq_out, go_out,
    tok, cot, tok_t, cot_t, docs, staged, w, joined, ctx, back, probs, q_rot, k_rot, grad_j,
    sq, rq, zs, zr, part, part_c, sum_c, recv_x, sum_x, recv_z, mixed,
    load_sem, ag_ss, ag_rs, agz_ss, agz_rs, rs_ss, rs_rs, rsz_ss, rsz_rs, tk_ss, tk_rs, mx_ss, mx_rs,
):
    blk = lax.axis_index("blk")
    ten = lax.axis_index("tensor")
    zh, y = blk // NY, blk % NY
    x, rest = ten // (NL * NC), ten % (NL * NC)
    lo, core = rest // NC, rest % NC
    rows = wq_in.shape[1]
    length = tok.shape[1]
    width = tok.shape[2]
    pick = zh % 2

    def at_z(k):
        return (((zh + k) % NZ) * NY + y, ten)

    def at_y(step):
        return (zh * NY + (y + step + NY) % NY, ten)

    def at_x(k):
        return (blk, ((x + k) % NX) * (NL * NC) + rest)

    up, down = at_y(1), at_y(-1)
    core_peer = (blk, ten + 1 - 2 * core)
    other_lo = ten + NC - 2 * NC * lo
    lo_peer = (blk, other_lo)
    other_blk = blk + NY - 2 * NY * pick
    partner = (other_blk, ten)
    partner_lo = (other_blk, other_lo)

    load_tok = pltpu.make_async_copy(tokens_hbm, tok.at[0], load_sem.at[0])
    load_cot = pltpu.make_async_copy(cot_hbm, cot.at[0], load_sem.at[1])
    load_tok.start()
    load_cot.start()

    barrier = pltpu.get_barrier_semaphore()
    peers = [at_z(k) for k in (1, 2, 3)] + [at_x(k) for k in (1, 2, 3)]
    peers += [up, down, core_peer, lo_peer, partner_lo]
    for peer in peers:
        pl.semaphore_signal(barrier, inc=1, device_id=peer, device_id_type=pl.DeviceIdType.MESH)

    def row_at(z, yy):
        return pl.ds(pl.multiple_of((z * NY + yy) * rows, 16), rows)

    for h in range(2):
        for c in range(3):
            staged[h, :, c * HD:(c + 1) * HD] = wq_in[c, :, h * HD:(h + 1) * HD]
        staged[h, :, 3 * HD:] = wo_in[:, h * HD:(h + 1) * HD]
    mine = row_at(zh, y)
    w[mine, :] = staged[pick]
    docs[0] = jnp.broadcast_to(doc_in[...], docs.shape[1:])
    load_tok.wait()
    load_cot.wait()
    pl.semaphore_wait(barrier, len(peers))

    def remote(src, dst, ss, rs, peer):
        return pltpu.make_async_remote_copy(
            src_ref=src, dst_ref=dst, send_sem=ss, recv_sem=rs,
            device_id=peer, device_id_type=pl.DeviceIdType.MESH,
        )

    def long(way, j):
        return j % 2 == way

    half = length // NC
    quarter = half // NX
    eighth = quarter // NL

    def place(c, xx=None, ll=None):
        if xx is None:
            return pl.ds(pl.multiple_of(c * half, 16), half)
        if ll is None:
            return pl.ds(pl.multiple_of(c * half + xx * quarter, 16), quarter)
        return pl.ds(pl.multiple_of(c * half + xx * quarter + ll * eighth, 16), eighth)

    def tk_copy(i, stage, got=False):
        a = (tok, cot)[i]
        if stage == 0:
            at = place(core, x, lo)
            return remote(a.at[0, at, :], a.at[1, at, :], tk_ss.at[i, 0], tk_rs.at[i, 0], partner)
        if stage == 1:
            at, peer = place(core, x, 1 - lo if got else lo), lo_peer
        elif stage == 5:
            at, peer = place(1 - core if got else core), core_peer
        else:
            k = stage - 1
            at, peer = place(core, (x - k + NX) % NX if got else x), at_x(k)
        return remote(a.at[1, at, :], a.at[1, at, :], tk_ss.at[i, stage], tk_rs.at[i, stage], peer)

    def tk_lo(i):
        tk_copy(i, 0).wait_recv()
        tk_copy(i, 1).start()

    def tk_x(i):
        tk_copy(i, 1, True).wait_recv()
        for stage in (2, 4, 3):
            tk_copy(i, stage).start()

    def tk_core(i):
        for stage in (2, 4, 3):
            tk_copy(i, stage, True).wait_recv()
        tk_copy(i, 5).start()

    def tk_end(i):
        tk_copy(i, 5, True).wait_recv()

    def tk_drain():
        for i in (0, 1):
            for stage in range(6):
                tk_copy(i, stage).wait_send()

    def doc_copy():
        return remote(docs.at[0], docs.at[1], tk_ss.at[0, 6], tk_rs.at[0, 6], partner)

    def ag_z(k):
        return remote(
            staged.at[(zh + k) % 2], w.at[mine, :], agz_ss.at[k], agz_rs.at[k], at_z(k)
        )

    def ag_y(way, s, j, got):
        sign = 1 if way == 0 else -1
        off = s + 1 if got else s
        here = row_at((zh - j + NZ) % NZ, (y - sign * off + 2 * NY) % NY)
        return remote(
            w.at[here, :], w.at[here, :], ag_ss.at[way, s, j], ag_rs.at[way, s, j],
            up if way == 0 else down,
        )

    def ag_step(j, s):
        if s == 0 and j > 0:
            here = row_at((zh - j + NZ) % NZ, y)
            remote(w.at[here, :], w.at[here, :], agz_ss.at[j], agz_rs.at[j], at_z(j)).wait_recv()
        for way in (0, 1):
            if s > 0:
                ag_y(way, s - 1, j, True).wait_recv()
            if s < 3 or long(way, j):
                ag_y(way, s, j, False).start()

    def ag_end():
        for j in range(NZ):
            for way in (0, 1):
                if long(way, j):
                    ag_y(way, 3, j, True).wait_recv()

    def ag_drain():
        for k in (1, 2, 3):
            ag_z(k).wait_send()
        for j in range(NZ):
            for way in (0, 1):
                for s in range(4):
                    if s < 3 or long(way, j):
                        ag_y(way, s, j, False).wait_send()

    def flip(a, a_t, m):
        def body(i, c):
            cols = pl.ds(pl.multiple_of(i * 256, 256), 256)
            a_t[cols, m * length:(m + 1) * length] = a[m, :, cols].T
            return c

        lax.fori_loop(0, width // 256, body, 0)

    cosine, sine = cos_in[...], sin_in[...]
    scale = 1.0 / math.sqrt(HD)

    def rows_of(m):
        return slice(m * length, (m + 1) * length)

    def project(m):
        joined[rows_of(m), :] = dot(tok[m], w[:, :3 * HD]).astype(BF16)

    def attend(m):
        qr = turned(joined[rows_of(m), :HD].astype(F32), cosine, sine)
        kr = turned(joined[rows_of(m), HD:2 * HD].astype(F32), cosine, sine)
        q_rot[m] = qr
        k_rot[m] = kr
        scores = lax.dot_general(qr, kr, NT, precision=HIGHEST, preferred_element_type=F32) * scale
        row = lax.broadcasted_iota(jnp.int32, (length, length), 0)
        col = lax.broadcasted_iota(jnp.int32, (length, length), 1)
        ids = jnp.broadcast_to(docs[m, :1, :], (length, length))
        allowed = (col <= row) & (ids == ids.T)
        scores = jnp.where(allowed, scores, -1e30)
        expo = jnp.exp(scores - jnp.max(scores, axis=1, keepdims=True))
        p = expo / jnp.sum(expo, axis=1, keepdims=True)
        probs[m] = p
        ctx[rows_of(m), :] = dot(p.astype(BF16), joined[rows_of(m), 2 * HD:]).astype(BF16)

    def retreat(m):
        p = probs[m]
        d_out = back[rows_of(m), :]
        d_val = jnp.dot(p.T, d_out.astype(F32), precision=HIGHEST, preferred_element_type=F32)
        d_p = dot_nt(d_out, joined[rows_of(m), 2 * HD:])
        d_s = p * (d_p - jnp.sum(p * d_p, axis=1, keepdims=True)) * scale
        d_q = jnp.dot(d_s, k_rot[m], precision=HIGHEST, preferred_element_type=F32)
        d_k = jnp.dot(d_s.T, q_rot[m], precision=HIGHEST, preferred_element_type=F32)
        grad_j[rows_of(m), :HD] = turned(d_q, cosine, -sine).astype(BF16)
        grad_j[rows_of(m), HD:2 * HD] = turned(d_k, cosine, -sine).astype(BF16)
        grad_j[rows_of(m), 2 * HD:] = d_val.astype(BF16)

    chunks = width // 512

    def outward(m):
        def body(i, c):
            r = pl.ds(pl.multiple_of(i * 512, 512), 512)
            part[m, :, r] = dot_nt(ctx[rows_of(m), :], w[r, 3 * HD:]).astype(BF16)
            return c

        lax.fori_loop(0, chunks, body, 0)

    def block_grad(z, yy):
        r = row_at(z, yy)
        return jnp.concatenate([dot(tok_t[r, :], grad_j[...]), dot(cot_t[r, :], ctx[...])], axis=1)

    def retract():
        for m in (0, 1):
            back[rows_of(m), :] = dot(cot[m], w[:, 3 * HD:]).astype(BF16)

    def rs_y(way, d, j):
        return remote(
            sq.at[way, d - 1, j], rq.at[way, d - 1, j], rs_ss.at[way, d - 1, j], rs_rs.at[way, d - 1, j],
            up if way == 0 else down,
        )

    def rs_step(j, u):
        d = 4 - u
        for way in (0, 1):
            if d == 4 and not long(way, j):
                continue
            sign = 1 if way == 0 else -1
            own = block_grad((zh - j + NZ) % NZ, (y + sign * d + NY) % NY)
            if d < 3 or (d == 3 and long(way, j)):
                rs_y(way, d + 1, j).wait_recv()
                own = own + rq[way, d, j].astype(F32)
            sq[way, d - 1, j] = own.astype(BF16)
            rs_y(way, d, j).start()

    def rs_here(j):
        own = block_grad((zh - j + NZ) % NZ, y)
        for way in (0, 1):
            rs_y(way, 1, j).wait_recv()
        return own + rq[0, 0, j].astype(F32) + rq[1, 0, j].astype(F32)

    def rs_z(j):
        return remote(zs.at[j], zr.at[j], rsz_ss.at[j], rsz_rs.at[j], at_z(NZ - j))

    def rs_out(j):
        zs[j] = rs_here(j).astype(BF16)
        rs_z(j).start()

    def rs_end():
        total = rs_here(0)
        for j in (1, 2, 3):
            rs_z(j).wait_recv()
        total = total + zr[2].astype(F32)
        across = zr[1].astype(F32) + zr[3].astype(F32)
        for at, value in ((pick, total), (1 - pick, across)):
            cols = pl.ds(pl.multiple_of(at * HD, HD), HD)
            for c in range(3):
                gq_out[c, :, cols] = value[:, c * HD:(c + 1) * HD]
            go_out[:, cols] = value[:, 3 * HD:]

    def rs_drain():
        for j in range(NZ):
            if j > 0:
                rs_z(j).wait_send()
            for way in (0, 1):
                for d in (1, 2, 3, 4):
                    if d < 4 or long(way, j):
                        rs_y(way, d, j).wait_send()

    def mx_core(m):
        return remote(part.at[m, place(1 - core), :], part_c.at[m], mx_ss.at[m, 0], mx_rs.at[m, 0], core_peer)

    def mx_x(m, k):
        away = pl.ds(pl.multiple_of(((x + k) % NX) * quarter, 16), quarter)
        return remote(sum_c.at[m, away, :], recv_x.at[m, k - 1], mx_ss.at[m, k], mx_rs.at[m, k], at_x(k))

    def mx_z(i):
        m, peer = ((0, lo_peer), (1, partner), (1, partner_lo))[i]
        at = pl.ds(pl.multiple_of((lo if i == 1 else 1 - lo) * eighth, 16), eighth)
        return remote(sum_x.at[m, at, :], recv_z.at[i], mx_ss.at[0, 4 + i], mx_rs.at[0, 4 + i], peer)

    def back_copy(stage, got=False):
        if stage == 0:
            at, peer = place(core, x, 1 - lo if got else lo), lo_peer
        elif stage == 4:
            at, peer = place(1 - core if got else core), core_peer
        else:
            at, peer = place(core, (x - stage + NX) % NX if got else x), at_x(stage)
        return remote(mixed.at[at, :], mixed.at[at, :], mx_ss.at[1, 4 + stage], mx_rs.at[1, 4 + stage], peer)

    def stage_x(m):
        mx_core(m).wait_recv()

        def body(i, c):
            r = pl.ds(pl.multiple_of(i * 16, 16), 16)
            there = pl.ds(pl.multiple_of(core * half + i * 16, 16), 16)
            sum_c[m, r, :] = (part[m, there, :].astype(F32) + part_c[m, r, :].astype(F32)).astype(BF16)
            return c

        lax.fori_loop(0, half // 16, body, 0)
        for k in (1, 3, 2):
            mx_x(m, k).start()

    def stage_z(m):
        total = sum_c[m, pl.ds(pl.multiple_of(x * quarter, 16), quarter), :].astype(F32)
        for k in (1, 3, 2):
            mx_x(m, k).wait_recv()
            total = total + recv_x[m, k - 1].astype(F32)
        sum_x[m] = total.astype(BF16)
        for i in ((0,), (1, 2))[m]:
            mx_z(i).start()

    def stage_back():
        total = sum_x[0, pl.ds(pl.multiple_of(lo * eighth, 16), eighth), :].astype(F32)
        for i in range(3):
            mx_z(i).wait_recv()
            total = total + recv_z[i].astype(F32)
        at = place(core, x, lo)
        mixed[at, :] = (tok[0, at, :].astype(F32) + total).astype(BF16)
        back_copy(0).start()

    def stage_back_x():
        back_copy(0, True).wait_recv()
        for k in (1, 3, 2):
            back_copy(k).start()

    def stage_back_core():
        for k in (1, 3, 2):
            back_copy(k, True).wait_recv()
        back_copy(4).start()

    def mx_drain():
        for m in (0, 1):
            mx_core(m).wait_send()
            for k in (1, 2, 3):
                mx_x(m, k).wait_send()
        for i in range(3):
            mx_z(i).wait_send()
        for stage in range(5):
            back_copy(stage).wait_send()

    def leave(got):
        at = place(1 - core if got else core)
        return pltpu.make_async_copy(mixed.at[at, :], mixed_out.at[at, :], load_sem.at[got])

    ag_step(0, 0)
    ag_z(1).start()
    ag_z(3).start()
    tk_copy(0, 0).start()
    ag_z(2).start()
    tk_copy(1, 0).start()
    doc_copy().start()
    flip(tok, tok_t, 0)
    ag_step(0, 1)
    flip(cot, cot_t, 0)
    ag_step(1, 0)
    ag_step(3, 0)
    tk_lo(0)
    ag_step(0, 2)
    ag_step(1, 1)
    ag_step(2, 0)
    tk_lo(1)
    ag_step(3, 1)
    tk_x(0)
    ag_step(0, 3)
    ag_step(1, 2)
    ag_step(2, 1)
    tk_x(1)
    ag_step(3, 2)
    ag_step(1, 3)
    ag_step(2, 2)
    ag_step(3, 3)
    ag_step(2, 3)
    tk_core(0)
    ag_end()

    project(0)
    attend(0)
    tk_end(0)
    project(1)
    doc_copy().wait_recv()
    attend(1)
    outward(1)
    mx_core(1).start()
    tk_core(1)
    outward(0)
    mx_core(0).start()
    flip(tok, tok_t, 1)
    stage_x(1)
    tk_end(1)
    stage_x(0)
    flip(cot, cot_t, 1)
    retract()
    retreat(0)
    retreat(1)
    stage_z(1)
    rs_step(2, 0)
    rs_step(1, 0)
    rs_step(3, 0)
    rs_step(2, 1)
    rs_step(1, 1)
    stage_z(0)
    rs_step(3, 1)
    rs_step(2, 2)
    rs_step(1, 2)
    rs_step(0, 0)
    rs_step(3, 2)
    stage_back()
    rs_step(2, 3)
    rs_step(1, 3)
    rs_step(0, 1)
    rs_out(2)
    stage_back_x()
    rs_step(3, 3)
    rs_out(1)
    rs_step(0, 2)
    rs_out(3)
    stage_back_core()
    leave(0).start()
    rs_step(0, 3)
    back_copy(4, True).wait_recv()
    leave(1).start()
    rs_end()

    ag_drain()
    tk_drain()
    doc_copy().wait_send()
    rs_drain()
    mx_drain()
    leave(0).wait()
    leave(1).wait()


def settle(*refs):
    ins, outs, held, sems = refs[:3], refs[3:6], refs[6:9], refs[9]
    parts = []
    for a in range(3):
        n = ins[a].shape[0]
        cut = n // 4 if a == 0 else n
        for at in range(0, n, cut):
            parts.append((a, pl.ds(at, cut)))
    loads = [
        pltpu.make_async_copy(ins[a].at[at], held[a].at[at], sems.at[0, i])
        for i, (a, at) in enumerate(parts)
    ]
    stores = [
        pltpu.make_async_copy(held[a].at[at], outs[a].at[at], sems.at[1, i])
        for i, (a, at) in enumerate(parts)
    ]
    for load in loads:
        load.start()
    for load, store in zip(loads, stores):
        load.wait()
        store.start()
    for store in stores:
        store.wait()


def local(tokens, doc_ids, qkv_weight, out_weight, cotangent):
    length, width = tokens.shape
    rows, _, feature = qkv_weight.shape
    block = 4 * HD
    frequency = 10000.0 ** (-2.0 * np.arange(HD // 2) / HD)
    angles = np.arange(length)[:, None] * frequency[None, :]
    cosine = jnp.asarray(np.concatenate([np.cos(angles), np.cos(angles)], axis=1), F32)
    sine = jnp.asarray(np.concatenate([-np.sin(angles), np.sin(angles)], axis=1), F32)
    vmem = pl.BlockSpec(memory_space=pltpu.VMEM)
    hbm = pl.BlockSpec(memory_space=pl.ANY)
    dma = pltpu.SemaphoreType.DMA
    half = length // NC
    quarter = half // NX
    mixed, grad_q, grad_o = pl.pallas_call(
        kernel,
        out_shape=(
            jax.ShapeDtypeStruct((length, width), BF16),
            jax.ShapeDtypeStruct((3, rows, feature), F32),
            jax.ShapeDtypeStruct((rows, feature), F32),
        ),
        in_specs=[hbm, hbm] + [vmem] * 5,
        out_specs=(hbm, vmem, vmem),
        scratch_shapes=[
            pltpu.VMEM((2, length, width), BF16),
            pltpu.VMEM((2, length, width), BF16),
            pltpu.VMEM((width, 2 * length), BF16),
            pltpu.VMEM((width, 2 * length), BF16),
            pltpu.VMEM((2, 8, length), jnp.int32),
            pltpu.VMEM((2, rows, block), BF16),
            pltpu.VMEM((width, block), BF16),
            pltpu.VMEM((2 * length, 3 * HD), BF16),
            pltpu.VMEM((2 * length, HD), BF16),
            pltpu.VMEM((2 * length, HD), BF16),
            pltpu.VMEM((2, length, length), F32),
            pltpu.VMEM((2, length, HD), F32),
            pltpu.VMEM((2, length, HD), F32),
            pltpu.VMEM((2 * length, 3 * HD), BF16),
            pltpu.VMEM((2, 4, NZ, rows, block), BF16),
            pltpu.VMEM((2, 4, NZ, rows, block), BF16),
            pltpu.VMEM((NZ, rows, block), BF16),
            pltpu.VMEM((NZ, rows, block), BF16),
            pltpu.VMEM((2, length, width), BF16),
            pltpu.VMEM((2, half, width), BF16),
            pltpu.VMEM((2, half, width), BF16),
            pltpu.VMEM((2, NX - 1, quarter, width), BF16),
            pltpu.VMEM((2, quarter, width), BF16),
            pltpu.VMEM((3, quarter // NL, width), BF16),
            pltpu.VMEM((length, width), BF16),
            dma((2,)),
            dma((2, 4, NZ)),
            dma((2, 4, NZ)),
            dma((NZ,)),
            dma((NZ,)),
            dma((2, 4, NZ)),
            dma((2, 4, NZ)),
            dma((NZ,)),
            dma((NZ,)),
            dma((2, 7)),
            dma((2, 7)),
            dma((2, 9)),
            dma((2, 9)),
        ],
        compiler_params=pltpu.CompilerParams(
            collective_id=0, has_side_effects=True, vmem_limit_bytes=56 * 1024 * 1024
        ),
        name="layer",
    )(
        tokens,
        cotangent,
        qkv_weight.transpose(1, 0, 2),
        out_weight.T,
        doc_ids.reshape(1, length),
        cosine,
        sine,
    )
    outs = (mixed, grad_q, grad_o)
    mixed, grad_q, grad_o = pl.pallas_call(
        settle,
        out_shape=tuple(jax.ShapeDtypeStruct(o.shape, o.dtype) for o in outs),
        in_specs=[hbm] * 3,
        out_specs=(hbm,) * 3,
        scratch_shapes=[pltpu.VMEM(o.shape, o.dtype) for o in outs] + [dma((2, 6))],
        name="settle",
    )(*outs)
    return mixed, grad_q.transpose(1, 0, 2), grad_o.T


def solution(mesh):
    placed = (
        P("blk", None),
        P("blk"),
        P("blk", None, "tensor"),
        P("tensor", "blk"),
        P("blk", None),
    )
    return jax.shard_map(
        local,
        mesh=mesh,
        in_specs=placed,
        out_specs=(P("blk", None), P("blk", None, "tensor"), P("tensor", "blk")),
        check_vma=False,
    )
```

```python
import math

import jax
import jax.numpy as jnp
import numpy as np
from jax import lax
from jax.experimental import pallas as pl
from jax.experimental.pallas import tpu as pltpu
from jax.sharding import PartitionSpec as P

HD = 128
NZ, NY = 4, 8
NX, NL, NC = 4, 2, 2
F32 = jnp.float32
BF16 = jnp.bfloat16
HIGHEST = lax.Precision.HIGHEST
NT = (((1,), (1,)), ((), ()))


def dot(a, b):
    return jnp.dot(a, b, preferred_element_type=F32)


def dot_nt(a, b):
    return lax.dot_general(a, b, NT, preferred_element_type=F32)


def turned(x, cosine, sine):
    half = x.shape[1] // 2
    swapped = jnp.concatenate([x[:, half:], x[:, :half]], axis=1)
    return x * cosine + swapped * sine


def kernel(
    tokens_hbm, cot_hbm, wq_in, wo_in, doc_in, cos_in, sin_in,
    mixed_out, gq_out, go_out,
    tok, cot, tok_t, cot_t, docs, staged, w, joined, ctx, back, probs, q_rot, k_rot, grad_j,
    sq, rq, zs, zr, part, part_c, sum_c, recv_x, sum_x, recv_z, mixed,
    load_sem, ag_ss, ag_rs, agz_ss, agz_rs, rs_ss, rs_rs, rsz_ss, rsz_rs, tk_ss, tk_rs, mx_ss, mx_rs,
):
    blk = lax.axis_index("blk")
    ten = lax.axis_index("tensor")
    zh, y = blk // NY, blk % NY
    x, rest = ten // (NL * NC), ten % (NL * NC)
    lo, core = rest // NC, rest % NC
    rows = wq_in.shape[1]
    length = tok.shape[1]
    width = tok.shape[2]
    pick = zh % 2

    def at_z(k):
        return (((zh + k) % NZ) * NY + y, ten)

    def at_y(step):
        return (zh * NY + (y + step + NY) % NY, ten)

    def at_x(k):
        return (blk, ((x + k) % NX) * (NL * NC) + rest)

    up, down = at_y(1), at_y(-1)
    core_peer = (blk, ten + 1 - 2 * core)
    other_lo = ten + NC - 2 * NC * lo
    lo_peer = (blk, other_lo)
    other_blk = blk + NY - 2 * NY * pick
    partner = (other_blk, ten)
    partner_lo = (other_blk, other_lo)

    load_tok = pltpu.make_async_copy(tokens_hbm, tok.at[0], load_sem.at[0])
    load_cot = pltpu.make_async_copy(cot_hbm, cot.at[0], load_sem.at[1])
    load_tok.start()
    load_cot.start()

    barrier = pltpu.get_barrier_semaphore()
    peers = [at_z(k) for k in (1, 2, 3)] + [at_x(k) for k in (1, 2, 3)]
    peers += [up, down, core_peer, lo_peer, partner_lo]
    for peer in peers:
        pl.semaphore_signal(barrier, inc=1, device_id=peer, device_id_type=pl.DeviceIdType.MESH)

    def row_at(z, yy):
        return pl.ds(pl.multiple_of((z * NY + yy) * rows, 16), rows)

    for h in range(2):
        for c in range(3):
            staged[h, :, c * HD:(c + 1) * HD] = wq_in[c, :, h * HD:(h + 1) * HD]
        staged[h, :, 3 * HD:] = wo_in[:, h * HD:(h + 1) * HD]
    mine = row_at(zh, y)
    w[mine, :] = staged[pick]
    docs[0] = jnp.broadcast_to(doc_in[...], docs.shape[1:])
    load_tok.wait()
    load_cot.wait()
    pl.semaphore_wait(barrier, len(peers))

    def remote(src, dst, ss, rs, peer):
        return pltpu.make_async_remote_copy(
            src_ref=src, dst_ref=dst, send_sem=ss, recv_sem=rs,
            device_id=peer, device_id_type=pl.DeviceIdType.MESH,
        )

    def long(way, j):
        return j % 2 == way

    half = length // NC
    quarter = half // NX
    eighth = quarter // NL

    def place(c, xx=None, ll=None):
        if xx is None:
            return pl.ds(pl.multiple_of(c * half, 16), half)
        if ll is None:
            return pl.ds(pl.multiple_of(c * half + xx * quarter, 16), quarter)
        return pl.ds(pl.multiple_of(c * half + xx * quarter + ll * eighth, 16), eighth)

    def tk_copy(i, stage, got=False):
        a = (tok, cot)[i]
        if stage == 0:
            at = place(core, x, lo)
            return remote(a.at[0, at, :], a.at[1, at, :], tk_ss.at[i, 0], tk_rs.at[i, 0], partner)
        if stage == 1:
            at, peer = place(core, x, 1 - lo if got else lo), lo_peer
        elif stage == 5:
            at, peer = place(1 - core if got else core), core_peer
        else:
            k = stage - 1
            at, peer = place(core, (x - k + NX) % NX if got else x), at_x(k)
        return remote(a.at[1, at, :], a.at[1, at, :], tk_ss.at[i, stage], tk_rs.at[i, stage], peer)

    def tk_lo(i):
        tk_copy(i, 0).wait_recv()
        tk_copy(i, 1).start()

    def tk_x(i):
        tk_copy(i, 1, True).wait_recv()
        for stage in (2, 4, 3):
            tk_copy(i, stage).start()

    def tk_core(i):
        for stage in (2, 4, 3):
            tk_copy(i, stage, True).wait_recv()
        tk_copy(i, 5).start()

    def tk_end(i):
        tk_copy(i, 5, True).wait_recv()

    def tk_drain():
        for i in (0, 1):
            for stage in range(6):
                tk_copy(i, stage).wait_send()

    def doc_copy():
        return remote(docs.at[0], docs.at[1], tk_ss.at[0, 6], tk_rs.at[0, 6], partner)

    def ag_z(k):
        return remote(
            staged.at[(zh + k) % 2], w.at[mine, :], agz_ss.at[k], agz_rs.at[k], at_z(k)
        )

    def ag_y(way, s, j, got):
        sign = 1 if way == 0 else -1
        off = s + 1 if got else s
        here = row_at((zh - j + NZ) % NZ, (y - sign * off + 2 * NY) % NY)
        return remote(
            w.at[here, :], w.at[here, :], ag_ss.at[way, s, j], ag_rs.at[way, s, j],
            up if way == 0 else down,
        )

    def ag_step(j, s):
        if s == 0 and j > 0:
            here = row_at((zh - j + NZ) % NZ, y)
            remote(w.at[here, :], w.at[here, :], agz_ss.at[j], agz_rs.at[j], at_z(j)).wait_recv()
        for way in (0, 1):
            if s > 0:
                ag_y(way, s - 1, j, True).wait_recv()
            if s < 3 or long(way, j):
                ag_y(way, s, j, False).start()

    def ag_end():
        for j in range(NZ):
            for way in (0, 1):
                if long(way, j):
                    ag_y(way, 3, j, True).wait_recv()

    def ag_drain():
        for k in (1, 2, 3):
            ag_z(k).wait_send()
        for j in range(NZ):
            for way in (0, 1):
                for s in range(4):
                    if s < 3 or long(way, j):
                        ag_y(way, s, j, False).wait_send()

    def flip(a, a_t, m):
        def body(i, c):
            cols = pl.ds(pl.multiple_of(i * 256, 256), 256)
            a_t[cols, m * length:(m + 1) * length] = a[m, :, cols].T
            return c

        lax.fori_loop(0, width // 256, body, 0)

    cosine, sine = cos_in[...], sin_in[...]
    scale = 1.0 / math.sqrt(HD)

    def rows_of(m):
        return slice(m * length, (m + 1) * length)

    def project(m):
        joined[rows_of(m), :] = dot(tok[m], w[:, :3 * HD]).astype(BF16)

    def attend(m):
        qr = turned(joined[rows_of(m), :HD].astype(F32), cosine, sine)
        kr = turned(joined[rows_of(m), HD:2 * HD].astype(F32), cosine, sine)
        q_rot[m] = qr
        k_rot[m] = kr
        scores = lax.dot_general(qr, kr, NT, precision=HIGHEST, preferred_element_type=F32) * scale
        row = lax.broadcasted_iota(jnp.int32, (length, length), 0)
        col = lax.broadcasted_iota(jnp.int32, (length, length), 1)
        ids = jnp.broadcast_to(docs[m, :1, :], (length, length))
        allowed = (col <= row) & (ids == ids.T)
        scores = jnp.where(allowed, scores, -1e30)
        expo = jnp.exp(scores - jnp.max(scores, axis=1, keepdims=True))
        p = expo / jnp.sum(expo, axis=1, keepdims=True)
        probs[m] = p
        ctx[rows_of(m), :] = dot(p.astype(BF16), joined[rows_of(m), 2 * HD:]).astype(BF16)

    def retreat(m):
        p = probs[m]
        d_out = back[rows_of(m), :]
        d_val = jnp.dot(p.T, d_out.astype(F32), precision=HIGHEST, preferred_element_type=F32)
        d_p = dot_nt(d_out, joined[rows_of(m), 2 * HD:])
        d_s = p * (d_p - jnp.sum(p * d_p, axis=1, keepdims=True)) * scale
        d_q = jnp.dot(d_s, k_rot[m], precision=HIGHEST, preferred_element_type=F32)
        d_k = jnp.dot(d_s.T, q_rot[m], precision=HIGHEST, preferred_element_type=F32)
        grad_j[rows_of(m), :HD] = turned(d_q, cosine, -sine).astype(BF16)
        grad_j[rows_of(m), HD:2 * HD] = turned(d_k, cosine, -sine).astype(BF16)
        grad_j[rows_of(m), 2 * HD:] = d_val.astype(BF16)

    chunks = width // 512

    def outward(m):
        def body(i, c):
            r = pl.ds(pl.multiple_of(i * 512, 512), 512)
            part[m, :, r] = dot_nt(ctx[rows_of(m), :], w[r, 3 * HD:]).astype(BF16)
            return c

        lax.fori_loop(0, chunks, body, 0)

    def block_grad(z, yy):
        r = row_at(z, yy)
        return jnp.concatenate([dot(tok_t[r, :], grad_j[...]), dot(cot_t[r, :], ctx[...])], axis=1)

    def retract():
        for m in (0, 1):
            back[rows_of(m), :] = dot(cot[m], w[:, 3 * HD:]).astype(BF16)

    def rs_y(way, d, j):
        return remote(
            sq.at[way, d - 1, j], rq.at[way, d - 1, j], rs_ss.at[way, d - 1, j], rs_rs.at[way, d - 1, j],
            up if way == 0 else down,
        )

    def rs_step(j, u):
        d = 4 - u
        for way in (0, 1):
            if d == 4 and not long(way, j):
                continue
            sign = 1 if way == 0 else -1
            own = block_grad((zh - j + NZ) % NZ, (y + sign * d + NY) % NY)
            if d < 3 or (d == 3 and long(way, j)):
                rs_y(way, d + 1, j).wait_recv()
                own = own + rq[way, d, j].astype(F32)
            sq[way, d - 1, j] = own.astype(BF16)
            rs_y(way, d, j).start()

    def rs_here(j):
        own = block_grad((zh - j + NZ) % NZ, y)
        for way in (0, 1):
            rs_y(way, 1, j).wait_recv()
        return own + rq[0, 0, j].astype(F32) + rq[1, 0, j].astype(F32)

    def rs_z(j):
        return remote(zs.at[j], zr.at[j], rsz_ss.at[j], rsz_rs.at[j], at_z(NZ - j))

    def rs_out(j):
        zs[j] = rs_here(j).astype(BF16)
        rs_z(j).start()

    def rs_end():
        total = rs_here(0)
        for j in (1, 2, 3):
            rs_z(j).wait_recv()
        total = total + zr[2].astype(F32)
        across = zr[1].astype(F32) + zr[3].astype(F32)
        for at, value in ((pick, total), (1 - pick, across)):
            cols = pl.ds(pl.multiple_of(at * HD, HD), HD)
            for c in range(3):
                gq_out[c, :, cols] = value[:, c * HD:(c + 1) * HD]
            go_out[:, cols] = value[:, 3 * HD:]

    def rs_drain():
        for j in range(NZ):
            if j > 0:
                rs_z(j).wait_send()
            for way in (0, 1):
                for d in (1, 2, 3, 4):
                    if d < 4 or long(way, j):
                        rs_y(way, d, j).wait_send()

    def mx_core(m):
        return remote(part.at[m, place(1 - core), :], part_c.at[m], mx_ss.at[m, 0], mx_rs.at[m, 0], core_peer)

    def mx_x(m, k):
        away = pl.ds(pl.multiple_of(((x + k) % NX) * quarter, 16), quarter)
        return remote(sum_c.at[m, away, :], recv_x.at[m, k - 1], mx_ss.at[m, k], mx_rs.at[m, k], at_x(k))

    def mx_z(i):
        m, peer = ((0, lo_peer), (1, partner), (1, partner_lo))[i]
        at = pl.ds(pl.multiple_of((lo if i == 1 else 1 - lo) * eighth, 16), eighth)
        return remote(sum_x.at[m, at, :], recv_z.at[i], mx_ss.at[0, 4 + i], mx_rs.at[0, 4 + i], peer)

    def back_copy(stage, got=False):
        if stage == 0:
            at, peer = place(core, x, 1 - lo if got else lo), lo_peer
        elif stage == 4:
            at, peer = place(1 - core if got else core), core_peer
        else:
            k, ll = (stage, lo) if stage < 4 else (stage - 4, 1 - lo)
            at, peer = place(core, (x - k + NX) % NX if got else x, ll), at_x(k)
        return remote(mixed.at[at, :], mixed.at[at, :], mx_ss.at[1, 4 + stage], mx_rs.at[1, 4 + stage], peer)

    def stage_x(m):
        mx_core(m).wait_recv()

        def body(i, c):
            r = pl.ds(pl.multiple_of(i * 16, 16), 16)
            there = pl.ds(pl.multiple_of(core * half + i * 16, 16), 16)
            sum_c[m, r, :] = (part[m, there, :].astype(F32) + part_c[m, r, :].astype(F32)).astype(BF16)
            return c

        lax.fori_loop(0, half // 16, body, 0)
        for k in (1, 3, 2):
            mx_x(m, k).start()

    def stage_z(m):
        total = sum_c[m, pl.ds(pl.multiple_of(x * quarter, 16), quarter), :].astype(F32)
        for k in (1, 3, 2):
            mx_x(m, k).wait_recv()
            total = total + recv_x[m, k - 1].astype(F32)
        sum_x[m] = total.astype(BF16)
        for i in ((0,), (1, 2))[m]:
            mx_z(i).start()

    def stage_back():
        total = sum_x[0, pl.ds(pl.multiple_of(lo * eighth, 16), eighth), :].astype(F32)
        for i in range(3):
            mx_z(i).wait_recv()
            total = total + recv_z[i].astype(F32)
        at = place(core, x, lo)
        mixed[at, :] = (tok[0, at, :].astype(F32) + total).astype(BF16)
        for stage in (0, 1, 3, 2):
            back_copy(stage).start()

    def stage_back_x():
        back_copy(0, True).wait_recv()
        for k in (1, 3, 2):
            back_copy(4 + k).start()

    def stage_back_core():
        for k in (1, 3, 2):
            back_copy(k, True).wait_recv()
            back_copy(4 + k, True).wait_recv()
        back_copy(4).start()

    def mx_drain():
        for m in (0, 1):
            mx_core(m).wait_send()
            for k in (1, 2, 3):
                mx_x(m, k).wait_send()
        for i in range(3):
            mx_z(i).wait_send()
        for stage in range(8):
            back_copy(stage).wait_send()

    def leave(got):
        at = place(1 - core if got else core)
        return pltpu.make_async_copy(mixed.at[at, :], mixed_out.at[at, :], load_sem.at[got])

    ag_step(0, 0)
    ag_z(1).start()
    ag_z(3).start()
    tk_copy(0, 0).start()
    ag_z(2).start()
    tk_copy(1, 0).start()
    doc_copy().start()
    flip(tok, tok_t, 0)
    ag_step(0, 1)
    flip(cot, cot_t, 0)
    ag_step(1, 0)
    ag_step(3, 0)
    tk_lo(0)
    ag_step(0, 2)
    ag_step(1, 1)
    ag_step(2, 0)
    tk_lo(1)
    ag_step(3, 1)
    tk_x(0)
    ag_step(0, 3)
    ag_step(1, 2)
    ag_step(2, 1)
    tk_x(1)
    ag_step(3, 2)
    ag_step(1, 3)
    ag_step(2, 2)
    ag_step(3, 3)
    ag_step(2, 3)
    tk_core(0)
    ag_end()

    project(0)
    attend(0)
    tk_end(0)
    project(1)
    doc_copy().wait_recv()
    attend(1)
    outward(1)
    mx_core(1).start()
    tk_core(1)
    outward(0)
    mx_core(0).start()
    flip(tok, tok_t, 1)
    stage_x(1)
    tk_end(1)
    stage_x(0)
    flip(cot, cot_t, 1)
    retract()
    retreat(0)
    retreat(1)
    stage_z(1)
    rs_step(2, 0)
    rs_step(1, 0)
    rs_step(3, 0)
    rs_step(2, 1)
    rs_step(1, 1)
    stage_z(0)
    rs_step(3, 1)
    rs_step(2, 2)
    rs_step(1, 2)
    rs_step(0, 0)
    rs_step(3, 2)
    stage_back()
    rs_step(2, 3)
    rs_step(1, 3)
    rs_step(0, 1)
    rs_out(2)
    stage_back_x()
    rs_step(3, 3)
    rs_out(1)
    rs_step(0, 2)
    rs_out(3)
    stage_back_core()
    leave(0).start()
    rs_step(0, 3)
    back_copy(4, True).wait_recv()
    leave(1).start()
    rs_end()

    ag_drain()
    tk_drain()
    doc_copy().wait_send()
    rs_drain()
    mx_drain()
    leave(0).wait()
    leave(1).wait()


def settle(*refs):
    ins, outs, held, sems = refs[:3], refs[3:6], refs[6:9], refs[9]
    parts = []
    for a in range(3):
        n = ins[a].shape[0]
        cut = n // 4 if a == 0 else n
        for at in range(0, n, cut):
            parts.append((a, pl.ds(at, cut)))
    loads = [
        pltpu.make_async_copy(ins[a].at[at], held[a].at[at], sems.at[0, i])
        for i, (a, at) in enumerate(parts)
    ]
    stores = [
        pltpu.make_async_copy(held[a].at[at], outs[a].at[at], sems.at[1, i])
        for i, (a, at) in enumerate(parts)
    ]
    for load in loads:
        load.start()
    for load, store in zip(loads, stores):
        load.wait()
        store.start()
    for store in stores:
        store.wait()


def local(tokens, doc_ids, qkv_weight, out_weight, cotangent):
    length, width = tokens.shape
    rows, _, feature = qkv_weight.shape
    block = 4 * HD
    frequency = 10000.0 ** (-2.0 * np.arange(HD // 2) / HD)
    angles = np.arange(length)[:, None] * frequency[None, :]
    cosine = jnp.asarray(np.concatenate([np.cos(angles), np.cos(angles)], axis=1), F32)
    sine = jnp.asarray(np.concatenate([-np.sin(angles), np.sin(angles)], axis=1), F32)
    vmem = pl.BlockSpec(memory_space=pltpu.VMEM)
    hbm = pl.BlockSpec(memory_space=pl.ANY)
    dma = pltpu.SemaphoreType.DMA
    half = length // NC
    quarter = half // NX
    mixed, grad_q, grad_o = pl.pallas_call(
        kernel,
        out_shape=(
            jax.ShapeDtypeStruct((length, width), BF16),
            jax.ShapeDtypeStruct((3, rows, feature), F32),
            jax.ShapeDtypeStruct((rows, feature), F32),
        ),
        in_specs=[hbm, hbm] + [vmem] * 5,
        out_specs=(hbm, vmem, vmem),
        scratch_shapes=[
            pltpu.VMEM((2, length, width), BF16),
            pltpu.VMEM((2, length, width), BF16),
            pltpu.VMEM((width, 2 * length), BF16),
            pltpu.VMEM((width, 2 * length), BF16),
            pltpu.VMEM((2, 8, length), jnp.int32),
            pltpu.VMEM((2, rows, block), BF16),
            pltpu.VMEM((width, block), BF16),
            pltpu.VMEM((2 * length, 3 * HD), BF16),
            pltpu.VMEM((2 * length, HD), BF16),
            pltpu.VMEM((2 * length, HD), BF16),
            pltpu.VMEM((2, length, length), F32),
            pltpu.VMEM((2, length, HD), F32),
            pltpu.VMEM((2, length, HD), F32),
            pltpu.VMEM((2 * length, 3 * HD), BF16),
            pltpu.VMEM((2, 4, NZ, rows, block), BF16),
            pltpu.VMEM((2, 4, NZ, rows, block), BF16),
            pltpu.VMEM((NZ, rows, block), BF16),
            pltpu.VMEM((NZ, rows, block), BF16),
            pltpu.VMEM((2, length, width), BF16),
            pltpu.VMEM((2, half, width), BF16),
            pltpu.VMEM((2, half, width), BF16),
            pltpu.VMEM((2, NX - 1, quarter, width), BF16),
            pltpu.VMEM((2, quarter, width), BF16),
            pltpu.VMEM((3, quarter // NL, width), BF16),
            pltpu.VMEM((length, width), BF16),
            dma((2,)),
            dma((2, 4, NZ)),
            dma((2, 4, NZ)),
            dma((NZ,)),
            dma((NZ,)),
            dma((2, 4, NZ)),
            dma((2, 4, NZ)),
            dma((NZ,)),
            dma((NZ,)),
            dma((2, 7)),
            dma((2, 7)),
            dma((2, 12)),
            dma((2, 12)),
        ],
        compiler_params=pltpu.CompilerParams(
            collective_id=0, has_side_effects=True, vmem_limit_bytes=56 * 1024 * 1024
        ),
        name="layer",
    )(
        tokens,
        cotangent,
        qkv_weight.transpose(1, 0, 2),
        out_weight.T,
        doc_ids.reshape(1, length),
        cosine,
        sine,
    )
    outs = (mixed, grad_q, grad_o)
    mixed, grad_q, grad_o = pl.pallas_call(
        settle,
        out_shape=tuple(jax.ShapeDtypeStruct(o.shape, o.dtype) for o in outs),
        in_specs=[hbm] * 3,
        out_specs=(hbm,) * 3,
        scratch_shapes=[pltpu.VMEM(o.shape, o.dtype) for o in outs] + [dma((2, 6))],
        name="settle",
    )(*outs)
    return mixed, grad_q.transpose(1, 0, 2), grad_o.T


def solution(mesh):
    placed = (
        P("blk", None),
        P("blk"),
        P("blk", None, "tensor"),
        P("tensor", "blk"),
        P("blk", None),
    )
    return jax.shard_map(
        local,
        mesh=mesh,
        in_specs=placed,
        out_specs=(P("blk", None), P("blk", None, "tensor"), P("tensor", "blk")),
        check_vma=False,
    )
```
